32 devices in a mesh: dp: 4 (over y, x), mp: 8 (over z, core).
Axes of the slice: x: 2, y: 2, z: 4, core: 2. Of those that a mesh axis runs over, the one named last changes fastest.
Arguments:
- tokens: bfloat16 [1280, 4096], P(('dp', 'mp')), may hold values from -6 to 6
- w_gate: bfloat16 [4096, 8192], P(None, 'mp'), may hold values from -0.09375 to 0.09375
- w_up: bfloat16 [4096, 8192], P(None, 'mp'), may hold values from -0.09375 to 0.09375
- w_down: bfloat16 [8192, 4096], P('mp'), may hold values from -0.0625 to 0.0625
- cotangent: bfloat16 [1280, 4096], P(('dp', 'mp')), may hold values from -6 to 6
Outputs:
- mixed: bfloat16 [1280, 4096], P(('dp', 'mp'))
- input_grad: bfloat16 [1280, 4096], P(('dp', 'mp'))
- grad_gate: bfloat16 [4096, 8192], P('dp', 'mp')
- grad_up: bfloat16 [4096, 8192], P('dp', 'mp')
- grad_down: bfloat16 [8192, 4096], P('mp', 'dp')
The draws below stay inside these ranges and needn't reach their ends.
All inputs are finite; a program needn't handle non-finite values.
Results may differ from the reference program's by a relative error of at most 0.019.
Values may be sent and summed in bfloat16 or wider, within the bound.
No kernel may reach another device: no remote copies, remote signals or barrier semaphores. Data moves between devices by JAX's collectives and lax.ppermute only.
A program may use at most 192 MiB of HBM per device.

```python
import jax
import jax.numpy as jnp
from jax import lax

D = 4096
FF = 8192
TOKENS = 1280
N_DP = 4


def strengthened(drawn, stream_key, source, target, parts, factor):
    owner, partner = [(jnp.arange(drawn.shape[dim]) // (drawn.shape[dim] // parts)).reshape([-1 if axis == dim else 1 for axis in range(drawn.ndim)]) for dim in (source, target)]
    chosen = jax.random.permutation(stream_key, parts)[partner]
    strong = (owner == chosen) | (owner == (partner + parts // 2) % parts)
    return jnp.where(strong, factor * drawn, drawn)


def steps_of(rng, dims, pieces, smallest, largest):
    level, own = 1.0, jax.random.fold_in(rng, 6)
    for axis_at, shards_of in pieces:
        heights = jnp.exp(jax.random.uniform(jax.random.fold_in(own, axis_at), (shards_of,), jnp.float32, smallest / len(pieces), largest / len(pieces)))
        level = level * jnp.repeat(heights, dims[axis_at] // shards_of).reshape([-1 if axis == axis_at else 1 for axis in range(len(dims))])
    return level


def centred(own_key, extent, width, most, cuts=(), held_as=jnp.bfloat16):
    drawn = width * jax.random.normal(own_key, extent, jnp.float32)
    if cuts:
        drawn = drawn * steps_of(own_key, extent, cuts, -0.22, 0.18)
    return jnp.clip(drawn, -most, most).astype(held_as)


def gaussian_with(stream_key, shape, spread, most, split, heavy, dtype=jnp.bfloat16):
    entries = spread * jax.random.normal(stream_key, shape, jnp.float32)
    if split:
        entries = entries * steps_of(stream_key, shape, split, -0.22, 0.18)
    return jnp.clip(strengthened(entries, jax.random.fold_in(stream_key, 3), *heavy), -most, most).astype(dtype)


def setup_inputs(seed: int = 0) -> dict:
    seeds = jax.random.split(jax.random.key(seed), 6)
    tokens = gaussian_with(seeds[0], (TOKENS, D), 1.0, 6.0, ((0, 32),), (0, 1, 32, 2.75))
    w_gate = centred(seeds[1], (D, FF), D ** -0.5, 0.09375, ((1, 8),))
    w_up = centred(seeds[2], (D, FF), D ** -0.5, 0.09375, ((1, 8),))
    w_down = centred(seeds[3], (FF, D), FF ** -0.5, 0.0625, ((0, 8),))
    cotangent = centred(seeds[4], (TOKENS, D), 1.0, 6.0, ((0, 32),))
    return {"tokens": tokens, "w_gate": w_gate, "w_up": w_up, "w_down": w_down, "cotangent": cotangent}


def group_sum(left, right):
    width_left = left.shape[1]
    width_right = right.shape[1]
    left_groups = left.reshape(N_DP, -1, width_left)
    right_groups = right.reshape(N_DP, -1, width_right)

    def step(total, pair):
        term = jnp.dot(pair[0].T, pair[1], preferred_element_type=jnp.float32)
        term = lax.optimization_barrier(term.astype(jnp.bfloat16)).astype(jnp.float32)
        return total + term, None

    total, unused = lax.scan(step, jnp.zeros((width_left, width_right), jnp.float32), (left_groups, right_groups))
    return total.astype(jnp.bfloat16)


def reference(tokens, w_gate, w_up, w_down, cotangent):
    gate = jnp.dot(tokens, w_gate, preferred_element_type=jnp.float32)
    up = jnp.dot(tokens, w_up, preferred_element_type=jnp.float32)
    swish = jax.nn.silu(gate)
    hidden = (swish * up).astype(jnp.bfloat16)
    mixed = jnp.dot(hidden, w_down, preferred_element_type=jnp.float32).astype(jnp.bfloat16)
    dhidden = jnp.dot(cotangent, w_down.T, preferred_element_type=jnp.float32)
    sigma = jax.nn.sigmoid(gate)
    dgate = (dhidden * up * sigma * (1.0 + gate * (1.0 - sigma))).astype(jnp.bfloat16)
    dup = (dhidden * swish).astype(jnp.bfloat16)
    input_grad = (jnp.dot(dgate, w_gate.T, preferred_element_type=jnp.float32)
                  + jnp.dot(dup, w_up.T, preferred_element_type=jnp.float32)).astype(jnp.bfloat16)
    grad_gate = group_sum(tokens, dgate)
    grad_up = group_sum(tokens, dup)
    grad_down = group_sum(hidden, cotangent)
    return mixed, input_grad, grad_gate, grad_up, grad_down
```

```python
import functools

import jax
import jax.numpy as jnp
from jax import lax
from jax.experimental import pallas as pl
from jax.experimental.pallas import tpu as pltpu
from jax.sharding import PartitionSpec as P

CORES = 2
MIB = 1 << 20


def contract_rows(left, right):
    return lax.dot_general(
        left, right, (((0,), (0,)), ((), ())), preferred_element_type=jnp.float32
    )


def contract_cols(left, right):
    return lax.dot_general(
        left, right, (((1,), (1,)), ((), ())), preferred_element_type=jnp.float32
    )


def product(left, right):
    return jnp.dot(left, right, preferred_element_type=jnp.float32)


def after(value, earlier):
    return lax.optimization_barrier((value, earlier))[0]


SMEM = pl.BlockSpec(memory_space=pltpu.SMEM)
ANY = pl.BlockSpec(memory_space=pl.ANY)


def call(body, steps, ins, in_specs, outs, out_specs, scratch=()):
    return pl.pallas_call(
        body,
        grid=(steps,),
        in_specs=in_specs,
        out_specs=out_specs,
        out_shape=outs,
        scratch_shapes=scratch,
        compiler_params=pltpu.CompilerParams(vmem_limit_bytes=56 * MIB),
        cost_estimate=pl.CostEstimate(flops=0, bytes_accessed=0, transcendentals=0),
    )(*ins)


def whole(array):
    return pl.BlockSpec(array.shape, lambda i: (0,) * len(array.shape))


def out_columns(rows, width):
    return jax.ShapeDtypeStruct((rows, width), jnp.bfloat16)


CHUNK = 64
SPLIT = 2


class Stream:
    def __init__(self, weights, axis, block):
        self.axis, self.block, self.count = axis, block, len(weights)
        self.steps = weights[0].shape[axis] // block
        shape = list(weights[0].shape)
        shape[axis] = block
        slots = (self.count, self.steps)
        self.scratch = (
            pltpu.VMEM((*slots, *shape), weights[0].dtype),
            pltpu.SemaphoreType.DMA((*slots, SPLIT)),
        )

    def copies(self, step, refs, held, sems):
        at = step * self.block
        at = pl.ds(at if isinstance(at, int) else pl.multiple_of(at, self.block), self.block)
        rows = held.shape[2] // SPLIT
        for w, ref in enumerate(refs):
            block = ref.at[:, at] if self.axis else ref.at[at]
            for part in range(SPLIT):
                some = pl.ds(part * rows, rows)
                yield pltpu.make_async_copy(
                    block.at[some], held.at[w, step, some], sems.at[w, step, part]
                )

    def begin(self, refs, held, sems, steps):
        for step in steps:
            for copy in self.copies(step, refs, held, sems):
                copy.start()

    def blocks(self, refs, held, sems):
        step = pl.program_id(0)
        for copy in self.copies(step, refs, held, sems):
            copy.wait()
        return [held[w, step] for w in range(self.count)]


class Gathered:
    def __init__(self, rows):
        self.rows = rows
        self.scratch = (
            pltpu.VMEM(rows.shape, rows.dtype),
            pltpu.SemaphoreType.DMA((rows.shape[0] // CHUNK,)),
        )

    def fill(self, ref, x_ref, sems, then):
        copies = []
        for i in range(x_ref.shape[0] // CHUNK):
            at = pl.ds(i * CHUNK, CHUNK)
            copies.append(pltpu.make_async_copy(ref.at[at], x_ref.at[at], sems.at[i]))
        for copy in copies:
            copy.start()
        then()
        for copy in copies:
            copy.wait()


def hand_out_body(orders, where_ref, rows_ref, *refs):
    *outs, sems = refs
    core, group = where_ref[1], where_ref[2]
    copies = []
    for out, j0, j1 in zip(outs, orders[0][1:], orders[1][1:]):
        half, width = out.shape
        at = (group ^ jnp.where(core == 0, j0, j1)) * width
        at = pl.ds(pl.multiple_of(at, width), width)
        rows = pl.ds(pl.multiple_of(core * half, half), half)
        copies.append(
            pltpu.make_async_copy(rows_ref.at[rows, at], out, sems.at[len(copies)])
        )
    for copy in copies:
        copy.start()
    for copy in copies:
        copy.wait()


def hand_out(where, rows, groups):
    block = out_columns(rows.shape[0] // CORES, rows.shape[1] // groups)
    count = groups - 1
    return call(
        functools.partial(hand_out_body, group_order(groups)),
        1,
        (where, rows),
        [SMEM, ANY],
        (block,) * count,
        (whole(block),) * count,
        (pltpu.SemaphoreType.DMA((count,)),),
    )


def forward_body(
    rows, weights, x_in, w_gate_ref, w_up_ref, hidden_ref, swish_ref, slope_ref, *scratch
):
    x_ref, x_sems, held, sems = scratch
    refs = (w_gate_ref, w_up_ref)

    @pl.when(pl.program_id(0) == 0)
    def _():
        weights.begin(refs, held, sems, [0])
        rest = range(1, weights.steps)
        rows.fill(x_in, x_ref, x_sems, lambda: weights.begin(refs, held, sems, rest))

    w_gate, w_up = weights.blocks(refs, held, sems)
    gate = product(x_ref[...], w_gate)
    up = product(x_ref[...], w_up)
    sigma = jax.nn.sigmoid(gate)
    swish = gate * sigma
    hidden_ref[...] = (swish * up).astype(hidden_ref.dtype)
    swish_ref[...] = swish
    slope_ref[...] = up * sigma * (1.0 + gate * (1.0 - sigma))


def forward(x, w_gate, w_up):
    rows, panel = x.shape[0], w_gate.shape[1]
    held, weights = Gathered(x), Stream((w_gate, w_up), 1, min(256, panel))
    out = pl.BlockSpec((rows, weights.block), lambda i: (0, i))
    kept = jax.ShapeDtypeStruct((rows, panel), jnp.float32)
    return call(
        functools.partial(forward_body, held, weights),
        weights.steps,
        (x, w_gate, w_up),
        [ANY] * 3,
        (out_columns(rows, panel), kept, kept),
        (out, out, out),
        held.scratch + weights.scratch,
    )


def project_body(weights, hidden_ref, w_ref, out_ref, held, sems):
    steps = range(weights.steps)
    pl.when(pl.program_id(0) == 0)(lambda: weights.begin((w_ref,), held, sems, steps))
    (w,) = weights.blocks((w_ref,), held, sems)
    out_ref[...] = product(hidden_ref[...], w).astype(out_ref.dtype)


def project(hidden, w_down):
    rows, depth = hidden.shape[0], w_down.shape[1]
    weights = Stream((w_down,), 1, min(1024, depth))
    return call(
        functools.partial(project_body, weights),
        weights.steps,
        (hidden, w_down),
        [whole(hidden), ANY],
        (jax.ShapeDtypeStruct((rows, depth), jnp.bfloat16),),
        (pl.BlockSpec((rows, weights.block), lambda i: (0, i)),),
        weights.scratch,
    )[0]


def backward_body(
    rows, weights, x_in, w_ref, swish_ref, slope_ref, dgate_ref, dup_ref, *scratch
):
    x_ref, x_sems, held, sems = scratch

    @pl.when(pl.program_id(0) == 0)
    def _():
        weights.begin((w_ref,), held, sems, [0])
        rest = range(1, weights.steps)
        rows.fill(
            x_in, x_ref, x_sems, lambda: weights.begin((w_ref,), held, sems, rest)
        )

    (w,) = weights.blocks((w_ref,), held, sems)
    dhidden = contract_cols(x_ref[...], w)
    dgate_ref[...] = (dhidden * slope_ref[...]).astype(dgate_ref.dtype)
    dup_ref[...] = (dhidden * swish_ref[...]).astype(dup_ref.dtype)


def backward(x, w_down, swish, slope):
    rows, panel = x.shape[0], w_down.shape[0]
    held, weights = Gathered(x), Stream((w_down,), 0, min(256, panel))
    part = pl.BlockSpec((rows, weights.block), lambda i: (0, i))
    return call(
        functools.partial(backward_body, held, weights),
        weights.steps,
        (x, w_down, swish, slope),
        [ANY, ANY, part, part],
        (out_columns(rows, panel),) * 2,
        (part, part),
        held.scratch + weights.scratch,
    )


def input_body(weights, dgate_ref, dup_ref, w_gate_ref, w_up_ref, out_ref, held, sems):
    refs = (w_gate_ref, w_up_ref)
    steps = range(weights.steps)
    pl.when(pl.program_id(0) == 0)(lambda: weights.begin(refs, held, sems, steps))
    w_gate, w_up = weights.blocks(refs, held, sems)
    total = contract_cols(dgate_ref[...], w_gate) + contract_cols(dup_ref[...], w_up)
    out_ref[...] = total.astype(out_ref.dtype)


def input_sum(dgate, dup, w_gate, w_up):
    rows, depth = dgate.shape[0], w_gate.shape[0]
    weights = Stream((w_gate, w_up), 0, min(512, depth))
    return call(
        functools.partial(input_body, weights),
        weights.steps,
        (dgate, dup, w_gate, w_up),
        [whole(dgate), whole(dup), ANY, ANY],
        (jax.ShapeDtypeStruct((rows, depth), jnp.bfloat16),),
        (pl.BlockSpec((rows, weights.block), lambda i: (0, i)),),
        weights.scratch,
    )[0]


def gradient_body(plans, counts, where_ref, *refs):
    out_ref, left_ref, right_ref, sems = refs[-4:]

    @pl.when(pl.program_id(0) == 0)
    def _():
        copies, first = [], 0
        for plan, count, held in zip(plans, counts, (left_ref, right_ref)):
            for source, at in plan(where_ref, *refs[first : first + count]):
                rows = source.shape[0]
                target = held.at[pl.ds(pl.multiple_of(at, 16), rows)]
                copies.append(
                    pltpu.make_async_copy(source, target, sems.at[len(copies)])
                )
            first += count
        for copy in copies:
            copy.start()
        for copy in copies:
            copy.wait()

    block = out_ref.shape[0]
    at = pl.ds(pl.multiple_of(pl.program_id(0) * block, block), block)
    total = contract_rows(left_ref[:, at], right_ref[...])
    out_ref[...] = total.astype(out_ref.dtype)


def gradient(where, plans, lefts, rights, depth, shape):
    block = min(256, shape[0])
    counts = (len(lefts), len(rights))
    return call(
        functools.partial(gradient_body, plans, counts),
        shape[0] // block,
        (where, *lefts, *rights),
        [SMEM] + [ANY] * sum(counts),
        (jax.ShapeDtypeStruct(shape, jnp.bfloat16),),
        (pl.BlockSpec((block, shape[1]), lambda i: (i, 0)),),
        (
            pltpu.VMEM((depth, shape[0]), jnp.bfloat16),
            pltpu.VMEM((depth, shape[1]), jnp.bfloat16),
            pltpu.SemaphoreType.DMA((32,)),
        ),
    )[0]


def pieces_plan(where_ref, *pieces):
    copies, at = [], 0
    for piece in pieces:
        copies.append((piece, at))
        at += piece.shape[0]
    return copies


def columns_plan(where_ref, gathered, *blocks):
    core, group, count = where_ref[1], where_ref[2], len(blocks) // 2
    rows, half, width = gathered.shape[0], *blocks[0].shape
    at = pl.ds(pl.multiple_of(group * width, width), width)
    copies = [(gathered.at[:, at], 0)]
    for label in range(1, count + 1):
        mine = blocks[label - 1]
        theirs = blocks[count + reverse(label, count + 1) - 1]
        copies.append((mine, label * rows + core * half))
        copies.append((theirs, label * rows + (1 - core) * half))
    return copies


def reverse(label, count):
    bits = count.bit_length() - 1
    return sum(1 << (bits - 1 - b) for b in range(bits) if label >> b & 1)


def swap_cores(value, chips):
    pairs = [(i, i ^ 1) for i in range(CORES * chips)]
    return lax.ppermute(value, "mp", pairs)


class Chain:
    def __init__(self, steps, *given):
        next(steps)
        self.steps, self.held, self.done = steps, given, False

    def advance(self):
        if not self.done:
            try:
                self.held = self.steps.send(self.held)
            except StopIteration as stop:
                self.held, self.done = stop.value, True


def fence(chains, *values):
    held, values = lax.optimization_barrier(([c.held for c in chains], values))
    for chain, value in zip(chains, held):
        chain.held = value
    return values


def group_order(groups):
    bits = [1 << b for b in range(groups.bit_length() - 1)]
    orders = []
    for c in range(CORES):
        held = [0]
        for bit in bits if c == 0 else bits[::-1]:
            held = held + [j ^ bit for j in held]
        orders.append(held)
    return orders


def group_pairs(ups, groups, members):
    return [
        (g * members + m, (g ^ ups[m % CORES]) * members + m)
        for g in range(groups)
        for m in range(members)
    ]


def gather_groups(groups, members, held, *plan):
    held += yield
    bits = [1 << b for b in range(groups.bit_length() - 1)]
    steps = list(zip(bits, bits[::-1]))
    for labels in plan:
        first = len(held)
        for label in labels:
            top = label.bit_length() - 1
            pairs = group_pairs(steps[top], groups, members)
            held.append(lax.ppermute(held[label - (1 << top)], ("dp", "mp"), pairs))
        held[first:] = yield held[first:]
    return ()


def exchange_groups(groups, members, mine, theirs):
    blocks = yield
    mine.update(enumerate(blocks, 1))
    bits = [1 << b for b in range(groups.bit_length() - 1)]
    ways = [group_pairs(ups, groups, members) for ups in zip(bits, bits[::-1])]
    left = {at: [w for b, w in zip(bits, ways) if at & b] for at in mine}
    while len(theirs) < len(mine):
        moved = [at for at in mine if left[at]]
        ready = [at for at in mine if not left[at] and at not in theirs]
        came = yield (
            [lax.ppermute(mine[at], ("dp", "mp"), left[at].pop(0)) for at in moved],
            [swap_cores(mine[at], members // CORES) for at in ready],
        )
        mine.update(zip(moved, came[0]))
        theirs.update(zip(ready, came[1]))
    return ()


def on_device(groups, members, tokens, w_gate, w_up, w_down, cotangent):
    group = lax.axis_index("dp")
    place = lax.axis_index("mp") // CORES
    core = lax.rem(lax.axis_index("mp"), CORES)
    where = jnp.stack([place, core, group])
    width = tokens.shape[1] // groups
    phases = groups.bit_length() - 1
    last = groups - 1

    def from_line(value):
        return lax.all_gather(value, "mp", axis=0, tiled=True)

    def over_line(value):
        return lax.psum_scatter(value, "mp", scatter_dimension=0, tiled=True)

    def over_groups(value, held, *plan):
        return Chain(gather_groups(groups, members, held, *plan), value)

    def exchange(blocks, mine, theirs):
        return Chain(exchange_groups(groups, members, mine, theirs), *blocks)

    def columns(gathered, mine, theirs):
        labels = range(1, groups)
        return (gathered, *(mine[at] for at in labels), *(theirs[at] for at in labels))

    upstream = from_line(cotangent)
    (gathered,) = fence([], from_line(tokens))

    blocks = hand_out(where, gathered, groups)
    all_hidden, mine, theirs = [], {}, {}
    across = exchange(blocks, mine, theirs)
    across.advance()
    hidden, swish, slope = fence(
        [across], *forward(after(gathered, blocks), w_gate, w_up)
    )

    hiddens = over_groups(hidden, all_hidden, [1], range(2, last), [last])
    hiddens.advance()
    for _ in range(phases - 1):
        across.advance()
    (partial,) = fence([hiddens, across], project(hidden, w_down))

    hiddens.advance()
    upstream, partial = fence([across], upstream, partial)
    mixed = over_line(partial)

    blocks = hand_out(where, upstream, groups)
    all_dgate, all_dup, mine_up, theirs_up = [], [], {}, {}
    across_up = exchange(blocks, mine_up, theirs_up)
    across_up.advance()
    dgate, dup = backward(after(upstream, blocks), w_down, swish, slope)
    dgate, dup = fence([hiddens, across, across_up], dgate, dup)

    gates = over_groups(dgate, all_dgate, [1], range(2, groups))
    ups = over_groups(dup, all_dup, [1], range(2, groups))
    hiddens.advance()
    gates.advance()
    for _ in range(phases - 1):
        across_up.advance()
    (partial,) = fence(
        [gates, hiddens, across, across_up], input_sum(dgate, dup, w_gate, w_up)
    )
    input_grad = over_line(partial)

    hiddens.advance()
    gates.advance()
    across.advance()
    across_up.advance()
    (mark,) = fence([gates, hiddens, across, across_up], partial)
    gates.advance()
    across.advance()
    across_up.advance()

    depth = groups * hidden.shape[0]
    shape = (width, hidden.shape[1])
    plans = (columns_plan, pieces_plan)
    ins = columns(gathered, mine, theirs)
    ups.advance()
    grad_gate = gradient(where, plans, after(ins, mark), all_dgate, depth, shape)
    (grad_gate,) = fence([ups], grad_gate)

    ups.advance()
    grad_down = gradient(
        where,
        plans[::-1],
        after(all_hidden, grad_gate),
        columns(upstream, mine_up, theirs_up),
        depth,
        shape[::-1],
    )
    (grad_down,) = fence([ups], grad_down)
    ups.advance()
    grad_up = gradient(where, plans, after(ins, grad_down), all_dup, depth, shape)
    return mixed, input_grad, grad_gate, grad_up, grad_down


def solution(mesh):
    in_specs = (
        P(("dp", "mp"), None),
        P(None, "mp"),
        P(None, "mp"),
        P("mp", None),
        P(("dp", "mp"), None),
    )
    out_specs = (
        P(("dp", "mp"), None),
        P(("dp", "mp"), None),
        P("dp", "mp"),
        P("dp", "mp"),
        P("mp", "dp"),
    )
    body = functools.partial(on_device, mesh.shape["dp"], mesh.shape["mp"])
    return jax.shard_map(
        body, mesh=mesh, in_specs=in_specs, out_specs=out_specs, check_vma=False
    )
```

```python
import functools

import jax
import jax.numpy as jnp
from jax import lax
from jax.experimental import pallas as pl
from jax.experimental.pallas import tpu as pltpu
from jax.sharding import PartitionSpec as P

CORES = 2
MIB = 1 << 20


def contract_rows(left, right):
    return lax.dot_general(
        left, right, (((0,), (0,)), ((), ())), preferred_element_type=jnp.float32
    )


def contract_cols(left, right):
    return lax.dot_general(
        left, right, (((1,), (1,)), ((), ())), preferred_element_type=jnp.float32
    )


def product(left, right):
    return jnp.dot(left, right, preferred_element_type=jnp.float32)


def after(value, earlier):
    return lax.optimization_barrier((value, earlier))[0]


SMEM = pl.BlockSpec(memory_space=pltpu.SMEM)
ANY = pl.BlockSpec(memory_space=pl.ANY)


def call(body, steps, ins, in_specs, outs, out_specs, scratch=()):
    return pl.pallas_call(
        body,
        grid=(steps,),
        in_specs=in_specs,
        out_specs=out_specs,
        out_shape=outs,
        scratch_shapes=scratch,
        compiler_params=pltpu.CompilerParams(vmem_limit_bytes=56 * MIB),
        cost_estimate=pl.CostEstimate(flops=0, bytes_accessed=0, transcendentals=0),
    )(*ins)


def whole(array):
    return pl.BlockSpec(array.shape, lambda i: (0,) * len(array.shape))


def out_columns(rows, width):
    return jax.ShapeDtypeStruct((rows, width), jnp.bfloat16)


CHUNK = 64
AHEAD = 2
SPLIT = 2


class Stream:
    def __init__(self, weights, axis, block):
        self.axis, self.block, self.count = axis, block, len(weights)
        self.steps = weights[0].shape[axis] // block
        shape = list(weights[0].shape)
        shape[axis] = block
        slots = (self.count, self.steps)
        self.scratch = (
            pltpu.VMEM((*slots, *shape), weights[0].dtype),
            pltpu.SemaphoreType.DMA((*slots, SPLIT)),
        )

    def copies(self, step, refs, held, sems):
        at = step * self.block
        at = pl.ds(at if isinstance(at, int) else pl.multiple_of(at, self.block), self.block)
        rows = held.shape[2] // SPLIT
        for w, ref in enumerate(refs):
            block = ref.at[:, at] if self.axis else ref.at[at]
            for part in range(SPLIT):
                some = pl.ds(part * rows, rows)
                yield pltpu.make_async_copy(
                    block.at[some], held.at[w, step, some], sems.at[w, step, part]
                )

    def begin(self, refs, held, sems, steps):
        for step in steps:
            for copy in self.copies(step, refs, held, sems):
                copy.start()

    def blocks(self, refs, held, sems):
        step = pl.program_id(0)

        @pl.when(step + AHEAD < self.steps)
        def _():
            for copy in self.copies(step + AHEAD, refs, held, sems):
                copy.start()

        for copy in self.copies(step, refs, held, sems):
            copy.wait()
        return [held[w, step] for w in range(self.count)]


class Gathered:
    def __init__(self, rows):
        self.rows = rows
        self.scratch = (
            pltpu.VMEM(rows.shape, rows.dtype),
            pltpu.SemaphoreType.DMA((rows.shape[0] // CHUNK,)),
        )

    def fill(self, ref, x_ref, sems, then):
        copies = []
        for i in range(x_ref.shape[0] // CHUNK):
            at = pl.ds(i * CHUNK, CHUNK)
            copies.append(pltpu.make_async_copy(ref.at[at], x_ref.at[at], sems.at[i]))
        for copy in copies:
            copy.start()
        then()
        for copy in copies:
            copy.wait()


def hand_out_body(orders, where_ref, rows_ref, *refs):
    *outs, sems = refs
    core, group = where_ref[1], where_ref[2]
    copies = []
    for out, j0, j1 in zip(outs, orders[0][1:], orders[1][1:]):
        half, width = out.shape
        at = (group ^ jnp.where(core == 0, j0, j1)) * width
        at = pl.ds(pl.multiple_of(at, width), width)
        rows = pl.ds(pl.multiple_of(core * half, half), half)
        copies.append(
            pltpu.make_async_copy(rows_ref.at[rows, at], out, sems.at[len(copies)])
        )
    for copy in copies:
        copy.start()
    for copy in copies:
        copy.wait()


def hand_out(where, rows, groups):
    block = out_columns(rows.shape[0] // CORES, rows.shape[1] // groups)
    count = groups - 1
    return call(
        functools.partial(hand_out_body, group_order(groups)),
        1,
        (where, rows),
        [SMEM, ANY],
        (block,) * count,
        (whole(block),) * count,
        (pltpu.SemaphoreType.DMA((count,)),),
    )


def forward_body(
    rows, weights, x_in, w_gate_ref, w_up_ref, hidden_ref, swish_ref, slope_ref, *scratch
):
    x_ref, x_sems, held, sems = scratch
    refs = (w_gate_ref, w_up_ref)

    @pl.when(pl.program_id(0) == 0)
    def _():
        weights.begin(refs, held, sems, [0])
        rest = range(1, min(AHEAD, weights.steps))
        rows.fill(x_in, x_ref, x_sems, lambda: weights.begin(refs, held, sems, rest))

    w_gate, w_up = weights.blocks(refs, held, sems)
    gate = product(x_ref[...], w_gate)
    up = product(x_ref[...], w_up)
    sigma = jax.nn.sigmoid(gate)
    swish = gate * sigma
    hidden_ref[...] = (swish * up).astype(hidden_ref.dtype)
    swish_ref[...] = swish
    slope_ref[...] = up * sigma * (1.0 + gate * (1.0 - sigma))


def forward(x, w_gate, w_up):
    rows, panel = x.shape[0], w_gate.shape[1]
    held, weights = Gathered(x), Stream((w_gate, w_up), 1, min(256, panel))
    out = pl.BlockSpec((rows, weights.block), lambda i: (0, i))
    kept = jax.ShapeDtypeStruct((rows, panel), jnp.float32)
    return call(
        functools.partial(forward_body, held, weights),
        weights.steps,
        (x, w_gate, w_up),
        [ANY] * 3,
        (out_columns(rows, panel), kept, kept),
        (out, out, out),
        held.scratch + weights.scratch,
    )


def project_body(weights, hidden_ref, w_ref, out_ref, held, sems):
    steps = range(min(AHEAD, weights.steps))
    pl.when(pl.program_id(0) == 0)(lambda: weights.begin((w_ref,), held, sems, steps))
    (w,) = weights.blocks((w_ref,), held, sems)
    out_ref[...] = product(hidden_ref[...], w).astype(out_ref.dtype)


def project(hidden, w_down):
    rows, depth = hidden.shape[0], w_down.shape[1]
    weights = Stream((w_down,), 1, min(1024, depth))
    return call(
        functools.partial(project_body, weights),
        weights.steps,
        (hidden, w_down),
        [whole(hidden), ANY],
        (jax.ShapeDtypeStruct((rows, depth), jnp.bfloat16),),
        (pl.BlockSpec((rows, weights.block), lambda i: (0, i)),),
        weights.scratch,
    )[0]


def backward_body(
    rows, weights, x_in, w_ref, swish_ref, slope_ref, dgate_ref, dup_ref, *scratch
):
    x_ref, x_sems, held, sems = scratch

    @pl.when(pl.program_id(0) == 0)
    def _():
        weights.begin((w_ref,), held, sems, [0])
        rest = range(1, min(AHEAD, weights.steps))
        rows.fill(
            x_in, x_ref, x_sems, lambda: weights.begin((w_ref,), held, sems, rest)
        )

    (w,) = weights.blocks((w_ref,), held, sems)
    dhidden = contract_cols(x_ref[...], w)
    dgate_ref[...] = (dhidden * slope_ref[...]).astype(dgate_ref.dtype)
    dup_ref[...] = (dhidden * swish_ref[...]).astype(dup_ref.dtype)


def backward(x, w_down, swish, slope):
    rows, panel = x.shape[0], w_down.shape[0]
    held, weights = Gathered(x), Stream((w_down,), 0, min(256, panel))
    part = pl.BlockSpec((rows, weights.block), lambda i: (0, i))
    return call(
        functools.partial(backward_body, held, weights),
        weights.steps,
        (x, w_down, swish, slope),
        [ANY, ANY, part, part],
        (out_columns(rows, panel),) * 2,
        (part, part),
        held.scratch + weights.scratch,
    )


def input_body(weights, dgate_ref, dup_ref, w_gate_ref, w_up_ref, out_ref, held, sems):
    refs = (w_gate_ref, w_up_ref)
    steps = range(min(AHEAD, weights.steps))
    pl.when(pl.program_id(0) == 0)(lambda: weights.begin(refs, held, sems, steps))
    w_gate, w_up = weights.blocks(refs, held, sems)
    total = contract_cols(dgate_ref[...], w_gate) + contract_cols(dup_ref[...], w_up)
    out_ref[...] = total.astype(out_ref.dtype)


def input_sum(dgate, dup, w_gate, w_up):
    rows, depth = dgate.shape[0], w_gate.shape[0]
    weights = Stream((w_gate, w_up), 0, min(1024, depth))
    return call(
        functools.partial(input_body, weights),
        weights.steps,
        (dgate, dup, w_gate, w_up),
        [whole(dgate), whole(dup), ANY, ANY],
        (jax.ShapeDtypeStruct((rows, depth), jnp.bfloat16),),
        (pl.BlockSpec((rows, weights.block), lambda i: (0, i)),),
        weights.scratch,
    )[0]


def gradient_body(plans, counts, where_ref, *refs):
    out_ref, left_ref, right_ref, sems = refs[-4:]

    @pl.when(pl.program_id(0) == 0)
    def _():
        copies, first = [], 0
        for plan, count, held in zip(plans, counts, (left_ref, right_ref)):
            for source, at in plan(where_ref, *refs[first : first + count]):
                rows = source.shape[0]
                target = held.at[pl.ds(pl.multiple_of(at, 16), rows)]
                copies.append(
                    pltpu.make_async_copy(source, target, sems.at[len(copies)])
                )
            first += count
        for copy in copies:
            copy.start()
        for copy in copies:
            copy.wait()

    block = out_ref.shape[0]
    at = pl.ds(pl.multiple_of(pl.program_id(0) * block, block), block)
    total = contract_rows(left_ref[:, at], right_ref[...])
    out_ref[...] = total.astype(out_ref.dtype)


def gradient(where, plans, lefts, rights, depth, shape):
    block = min(256, shape[0])
    counts = (len(lefts), len(rights))
    return call(
        functools.partial(gradient_body, plans, counts),
        shape[0] // block,
        (where, *lefts, *rights),
        [SMEM] + [ANY] * sum(counts),
        (jax.ShapeDtypeStruct(shape, jnp.bfloat16),),
        (pl.BlockSpec((block, shape[1]), lambda i: (i, 0)),),
        (
            pltpu.VMEM((depth, shape[0]), jnp.bfloat16),
            pltpu.VMEM((depth, shape[1]), jnp.bfloat16),
            pltpu.SemaphoreType.DMA((32,)),
        ),
    )[0]


def pieces_plan(where_ref, *pieces):
    copies, at = [], 0
    for piece in pieces:
        copies.append((piece, at))
        at += piece.shape[0]
    return copies


def columns_plan(where_ref, gathered, *blocks):
    core, group, count = where_ref[1], where_ref[2], len(blocks) // 2
    rows, half, width = gathered.shape[0], *blocks[0].shape
    at = pl.ds(pl.multiple_of(group * width, width), width)
    copies = [(gathered.at[:, at], 0)]
    for label in range(1, count + 1):
        mine = blocks[label - 1]
        theirs = blocks[count + reverse(label, count + 1) - 1]
        copies.append((mine, label * rows + core * half))
        copies.append((theirs, label * rows + (1 - core) * half))
    return copies


def reverse(label, count):
    bits = count.bit_length() - 1
    return sum(1 << (bits - 1 - b) for b in range(bits) if label >> b & 1)


def swap_cores(value, chips):
    pairs = [(i, i ^ 1) for i in range(CORES * chips)]
    return lax.ppermute(value, "mp", pairs)


class Chain:
    def __init__(self, steps, *given):
        next(steps)
        self.steps, self.held, self.done = steps, given, False

    def advance(self):
        if not self.done:
            try:
                self.held = self.steps.send(self.held)
            except StopIteration as stop:
                self.held, self.done = stop.value, True


def fence(chains, *values):
    held, values = lax.optimization_barrier(([c.held for c in chains], values))
    for chain, value in zip(chains, held):
        chain.held = value
    return values


def group_order(groups):
    bits = [1 << b for b in range(groups.bit_length() - 1)]
    orders = []
    for c in range(CORES):
        held = [0]
        for bit in bits if c == 0 else bits[::-1]:
            held = held + [j ^ bit for j in held]
        orders.append(held)
    return orders


def group_pairs(ups, groups, members):
    return [
        (g * members + m, (g ^ ups[m % CORES]) * members + m)
        for g in range(groups)
        for m in range(members)
    ]


def gather_groups(groups, members, held, *plan):
    held += yield
    bits = [1 << b for b in range(groups.bit_length() - 1)]
    steps = list(zip(bits, bits[::-1]))
    for labels in plan:
        first = len(held)
        for label in labels:
            top = label.bit_length() - 1
            pairs = group_pairs(steps[top], groups, members)
            held.append(lax.ppermute(held[label - (1 << top)], ("dp", "mp"), pairs))
        held[first:] = yield held[first:]
    return ()


def exchange_groups(groups, members, mine, theirs):
    blocks = yield
    mine.update(enumerate(blocks, 1))
    bits = [1 << b for b in range(groups.bit_length() - 1)]
    ways = [group_pairs(ups, groups, members) for ups in zip(bits, bits[::-1])]
    left = {at: [w for b, w in zip(bits, ways) if at & b] for at in mine}
    while len(theirs) < len(mine):
        moved = [at for at in mine if left[at]]
        ready = [at for at in mine if not left[at] and at not in theirs]
        came = yield (
            [lax.ppermute(mine[at], ("dp", "mp"), left[at].pop(0)) for at in moved],
            [swap_cores(mine[at], members // CORES) for at in ready],
        )
        mine.update(zip(moved, came[0]))
        theirs.update(zip(ready, came[1]))
    return ()


def on_device(groups, members, tokens, w_gate, w_up, w_down, cotangent):
    group = lax.axis_index("dp")
    place = lax.axis_index("mp") // CORES
    core = lax.rem(lax.axis_index("mp"), CORES)
    where = jnp.stack([place, core, group])
    width = tokens.shape[1] // groups
    phases = groups.bit_length() - 1
    last = groups - 1

    def from_line(value):
        return lax.all_gather(value, "mp", axis=0, tiled=True)

    def over_line(value):
        return lax.psum_scatter(value, "mp", scatter_dimension=0, tiled=True)

    def over_groups(value, held, *plan):
        return Chain(gather_groups(groups, members, held, *plan), value)

    def exchange(blocks, mine, theirs):
        return Chain(exchange_groups(groups, members, mine, theirs), *blocks)

    def columns(gathered, mine, theirs):
        labels = range(1, groups)
        return (gathered, *(mine[at] for at in labels), *(theirs[at] for at in labels))

    upstream = from_line(cotangent)
    (gathered,) = fence([], from_line(tokens))

    blocks = hand_out(where, gathered, groups)
    all_hidden, mine, theirs = [], {}, {}
    across = exchange(blocks, mine, theirs)
    across.advance()
    hidden, swish, slope = fence(
        [across], *forward(after(gathered, blocks), w_gate, w_up)
    )

    hiddens = over_groups(hidden, all_hidden, [1], range(2, last), [last])
    hiddens.advance()
    for _ in range(phases - 1):
        across.advance()
    (partial,) = fence([hiddens, across], project(hidden, w_down))

    hiddens.advance()
    upstream, partial = fence([across], upstream, partial)
    mixed = over_line(partial)

    blocks = hand_out(where, upstream, groups)
    all_dgate, all_dup, mine_up, theirs_up = [], [], {}, {}
    across_up = exchange(blocks, mine_up, theirs_up)
    across_up.advance()
    dgate, dup = backward(after(upstream, blocks), w_down, swish, slope)
    dgate, dup = fence([hiddens, across, across_up], dgate, dup)

    gates = over_groups(dgate, all_dgate, [1], range(2, groups))
    ups = over_groups(dup, all_dup, [1], range(2, groups))
    hiddens.advance()
    gates.advance()
    for _ in range(phases - 1):
        across_up.advance()
    (partial,) = fence(
        [gates, hiddens, across, across_up], input_sum(dgate, dup, w_gate, w_up)
    )
    input_grad = over_line(partial)

    hiddens.advance()
    gates.advance()
    ups.advance()
    across.advance()
    across_up.advance()
    (mark,) = fence([hiddens, across, across_up], partial)
    across.advance()
    across_up.advance()

    depth = groups * hidden.shape[0]
    shape = (width, hidden.shape[1])
    plans = (columns_plan, pieces_plan)
    grad_down = gradient(
        where,
        plans[::-1],
        after(all_hidden, mark),
        columns(upstream, mine_up, theirs_up),
        depth,
        shape[::-1],
    )
    (grad_down,) = fence([gates, ups], grad_down)
    gates.advance()

    ups.advance()
    ins = after(columns(gathered, mine, theirs), grad_down)
    grad_gate = gradient(where, plans, ins, all_dgate, depth, shape)
    (grad_gate,) = fence([ups], grad_gate)
    ups.advance()
    grad_up = gradient(where, plans, after(ins, grad_gate), all_dup, depth, shape)
    return mixed, input_grad, grad_gate, grad_up, grad_down


def solution(mesh):
    in_specs = (
        P(("dp", "mp"), None),
        P(None, "mp"),
        P(None, "mp"),
        P("mp", None),
        P(("dp", "mp"), None),
    )
    out_specs = (
        P(("dp", "mp"), None),
        P(("dp", "mp"), None),
        P("dp", "mp"),
        P("dp", "mp"),
        P("mp", "dp"),
    )
    body = functools.partial(on_device, mesh.shape["dp"], mesh.shape["mp"])
    return jax.shard_map(
        body, mesh=mesh, in_specs=in_specs, out_specs=out_specs, check_vma=False
    )
```

```python
import functools

import jax
import jax.numpy as jnp
from jax import lax
from jax.experimental import pallas as pl
from jax.experimental.pallas import tpu as pltpu
from jax.sharding import PartitionSpec as P

CORES = 2
MIB = 1 << 20


def contract_rows(left, right):
    return lax.dot_general(
        left, right, (((0,), (0,)), ((), ())), preferred_element_type=jnp.float32
    )


def contract_cols(left, right):
    return lax.dot_general(
        left, right, (((1,), (1,)), ((), ())), preferred_element_type=jnp.float32
    )


def product(left, right):
    return jnp.dot(left, right, preferred_element_type=jnp.float32)


def after(value, earlier):
    return lax.optimization_barrier((value, earlier))[0]


SMEM = pl.BlockSpec(memory_space=pltpu.SMEM)
ANY = pl.BlockSpec(memory_space=pl.ANY)


def call(body, steps, ins, in_specs, outs, out_specs, scratch=()):
    return pl.pallas_call(
        body,
        grid=(steps,),
        in_specs=in_specs,
        out_specs=out_specs,
        out_shape=outs,
        scratch_shapes=scratch,
        compiler_params=pltpu.CompilerParams(vmem_limit_bytes=56 * MIB),
        cost_estimate=pl.CostEstimate(flops=0, bytes_accessed=0, transcendentals=0),
    )(*ins)


def whole(array):
    return pl.BlockSpec(array.shape, lambda i: (0,) * len(array.shape))


def out_columns(rows, width):
    return jax.ShapeDtypeStruct((rows, width), jnp.bfloat16)


CHUNK = 64
AHEAD = 2
SPLIT = 2


class Stream:
    def __init__(self, weights, axis, block):
        self.axis, self.block, self.count = axis, block, len(weights)
        self.steps = weights[0].shape[axis] // block
        shape = list(weights[0].shape)
        shape[axis] = block
        slots = (self.count, self.steps)
        self.scratch = (
            pltpu.VMEM((*slots, *shape), weights[0].dtype),
            pltpu.SemaphoreType.DMA((*slots, SPLIT)),
        )

    def copies(self, step, refs, held, sems):
        at = step * self.block
        at = pl.ds(at if isinstance(at, int) else pl.multiple_of(at, self.block), self.block)
        rows = held.shape[2] // SPLIT
        for w, ref in enumerate(refs):
            block = ref.at[:, at] if self.axis else ref.at[at]
            for part in range(SPLIT):
                some = pl.ds(part * rows, rows)
                yield pltpu.make_async_copy(
                    block.at[some], held.at[w, step, some], sems.at[w, step, part]
                )

    def begin(self, refs, held, sems, steps):
        for step in steps:
            for copy in self.copies(step, refs, held, sems):
                copy.start()

    def blocks(self, refs, held, sems):
        step = pl.program_id(0)

        @pl.when(step + AHEAD < self.steps)
        def _():
            for copy in self.copies(step + AHEAD, refs, held, sems):
                copy.start()

        for copy in self.copies(step, refs, held, sems):
            copy.wait()
        return [held[w, step] for w in range(self.count)]


class Gathered:
    def __init__(self, rows):
        self.rows = rows
        self.scratch = (
            pltpu.VMEM(rows.shape, rows.dtype),
            pltpu.SemaphoreType.DMA((rows.shape[0] // CHUNK,)),
        )

    def fill(self, ref, x_ref, sems, then):
        copies = []
        for i in range(x_ref.shape[0] // CHUNK):
            at = pl.ds(i * CHUNK, CHUNK)
            copies.append(pltpu.make_async_copy(ref.at[at], x_ref.at[at], sems.at[i]))
        for copy in copies:
            copy.start()
        then()
        for copy in copies:
            copy.wait()


def hand_out_body(orders, where_ref, rows_ref, *refs):
    *outs, sems = refs
    core, group = where_ref[1], where_ref[2]
    copies = []
    for out, j0, j1 in zip(outs, orders[0][1:], orders[1][1:]):
        half, width = out.shape
        at = (group ^ jnp.where(core == 0, j0, j1)) * width
        at = pl.ds(pl.multiple_of(at, width), width)
        rows = pl.ds(pl.multiple_of(core * half, half), half)
        copies.append(
            pltpu.make_async_copy(rows_ref.at[rows, at], out, sems.at[len(copies)])
        )
    for copy in copies:
        copy.start()
    for copy in copies:
        copy.wait()


def hand_out(where, rows, groups):
    block = out_columns(rows.shape[0] // CORES, rows.shape[1] // groups)
    count = groups - 1
    return call(
        functools.partial(hand_out_body, group_order(groups)),
        1,
        (where, rows),
        [SMEM, ANY],
        (block,) * count,
        (whole(block),) * count,
        (pltpu.SemaphoreType.DMA((count,)),),
    )


def forward_body(
    rows, weights, x_in, w_gate_ref, w_up_ref, hidden_ref, swish_ref, slope_ref, *scratch
):
    x_ref, x_sems, held, sems = scratch
    refs = (w_gate_ref, w_up_ref)

    @pl.when(pl.program_id(0) == 0)
    def _():
        weights.begin(refs, held, sems, [0])
        rest = range(1, min(AHEAD, weights.steps))
        rows.fill(x_in, x_ref, x_sems, lambda: weights.begin(refs, held, sems, rest))

    w_gate, w_up = weights.blocks(refs, held, sems)
    gate = product(x_ref[...], w_gate)
    up = product(x_ref[...], w_up)
    sigma = jax.nn.sigmoid(gate)
    swish = gate * sigma
    hidden_ref[...] = (swish * up).astype(hidden_ref.dtype)
    swish_ref[...] = swish
    slope_ref[...] = up * sigma * (1.0 + gate * (1.0 - sigma))


def forward(x, w_gate, w_up):
    rows, panel = x.shape[0], w_gate.shape[1]
    held, weights = Gathered(x), Stream((w_gate, w_up), 1, min(256, panel))
    out = pl.BlockSpec((rows, weights.block), lambda i: (0, i))
    kept = jax.ShapeDtypeStruct((rows, panel), jnp.float32)
    return call(
        functools.partial(forward_body, held, weights),
        weights.steps,
        (x, w_gate, w_up),
        [ANY] * 3,
        (out_columns(rows, panel), kept, kept),
        (out, out, out),
        held.scratch + weights.scratch,
    )


def project_body(weights, hidden_ref, w_ref, out_ref, held, sems):
    steps = range(min(AHEAD, weights.steps))
    pl.when(pl.program_id(0) == 0)(lambda: weights.begin((w_ref,), held, sems, steps))
    (w,) = weights.blocks((w_ref,), held, sems)
    out_ref[...] = product(hidden_ref[...], w).astype(out_ref.dtype)


def project(hidden, w_down):
    rows, depth = hidden.shape[0], w_down.shape[1]
    weights = Stream((w_down,), 1, min(1024, depth))
    return call(
        functools.partial(project_body, weights),
        weights.steps,
        (hidden, w_down),
        [whole(hidden), ANY],
        (jax.ShapeDtypeStruct((rows, depth), jnp.bfloat16),),
        (pl.BlockSpec((rows, weights.block), lambda i: (0, i)),),
        weights.scratch,
    )[0]


def backward_body(
    rows, weights, x_in, w_ref, swish_ref, slope_ref, dgate_ref, dup_ref, *scratch
):
    x_ref, x_sems, held, sems = scratch

    @pl.when(pl.program_id(0) == 0)
    def _():
        weights.begin((w_ref,), held, sems, [0])
        rest = range(1, min(AHEAD, weights.steps))
        rows.fill(
            x_in, x_ref, x_sems, lambda: weights.begin((w_ref,), held, sems, rest)
        )

    (w,) = weights.blocks((w_ref,), held, sems)
    dhidden = contract_cols(x_ref[...], w)
    dgate_ref[...] = (dhidden * slope_ref[...]).astype(dgate_ref.dtype)
    dup_ref[...] = (dhidden * swish_ref[...]).astype(dup_ref.dtype)


def backward(x, w_down, swish, slope):
    rows, panel = x.shape[0], w_down.shape[0]
    held, weights = Gathered(x), Stream((w_down,), 0, min(256, panel))
    part = pl.BlockSpec((rows, weights.block), lambda i: (0, i))
    return call(
        functools.partial(backward_body, held, weights),
        weights.steps,
        (x, w_down, swish, slope),
        [ANY, ANY, part, part],
        (out_columns(rows, panel),) * 2,
        (part, part),
        held.scratch + weights.scratch,
    )


def input_body(weights, dgate_ref, dup_ref, w_gate_ref, w_up_ref, out_ref, held, sems):
    refs = (w_gate_ref, w_up_ref)
    steps = range(min(AHEAD, weights.steps))
    pl.when(pl.program_id(0) == 0)(lambda: weights.begin(refs, held, sems, steps))
    w_gate, w_up = weights.blocks(refs, held, sems)
    total = contract_cols(dgate_ref[...], w_gate) + contract_cols(dup_ref[...], w_up)
    out_ref[...] = total.astype(out_ref.dtype)


def input_sum(dgate, dup, w_gate, w_up):
    rows, depth = dgate.shape[0], w_gate.shape[0]
    weights = Stream((w_gate, w_up), 0, min(1024, depth))
    return call(
        functools.partial(input_body, weights),
        weights.steps,
        (dgate, dup, w_gate, w_up),
        [whole(dgate), whole(dup), ANY, ANY],
        (jax.ShapeDtypeStruct((rows, depth), jnp.bfloat16),),
        (pl.BlockSpec((rows, weights.block), lambda i: (0, i)),),
        weights.scratch,
    )[0]


def gradient_body(plans, counts, where_ref, *refs):
    out_ref, left_ref, right_ref, sems = refs[-4:]

    @pl.when(pl.program_id(0) == 0)
    def _():
        copies, first = [], 0
        for plan, count, held in zip(plans, counts, (left_ref, right_ref)):
            for source, at in plan(where_ref, *refs[first : first + count]):
                rows = source.shape[0]
                target = held.at[pl.ds(pl.multiple_of(at, 16), rows)]
                copies.append(
                    pltpu.make_async_copy(source, target, sems.at[len(copies)])
                )
            first += count
        for copy in copies:
            copy.start()
        for copy in copies:
            copy.wait()

    block = out_ref.shape[0]
    at = pl.ds(pl.multiple_of(pl.program_id(0) * block, block), block)
    total = contract_rows(left_ref[:, at], right_ref[...])
    out_ref[...] = total.astype(out_ref.dtype)


def gradient(where, plans, lefts, rights, depth, shape):
    block = min(256, shape[0])
    counts = (len(lefts), len(rights))
    return call(
        functools.partial(gradient_body, plans, counts),
        shape[0] // block,
        (where, *lefts, *rights),
        [SMEM] + [ANY] * sum(counts),
        (jax.ShapeDtypeStruct(shape, jnp.bfloat16),),
        (pl.BlockSpec((block, shape[1]), lambda i: (i, 0)),),
        (
            pltpu.VMEM((depth, shape[0]), jnp.bfloat16),
            pltpu.VMEM((depth, shape[1]), jnp.bfloat16),
            pltpu.SemaphoreType.DMA((32,)),
        ),
    )[0]


def pieces_plan(where_ref, *pieces):
    copies, at = [], 0
    for piece in pieces:
        copies.append((piece, at))
        at += piece.shape[0]
    return copies


def columns_plan(where_ref, gathered, *blocks):
    core, group, count = where_ref[1], where_ref[2], len(blocks) // 2
    rows, half, width = gathered.shape[0], *blocks[0].shape
    at = pl.ds(pl.multiple_of(group * width, width), width)
    copies = [(gathered.at[:, at], 0)]
    for label in range(1, count + 1):
        mine = blocks[label - 1]
        theirs = blocks[count + reverse(label, count + 1) - 1]
        copies.append((mine, label * rows + core * half))
        copies.append((theirs, label * rows + (1 - core) * half))
    return copies


def reverse(label, count):
    bits = count.bit_length() - 1
    return sum(1 << (bits - 1 - b) for b in range(bits) if label >> b & 1)


def swap_cores(value, chips):
    pairs = [(i, i ^ 1) for i in range(CORES * chips)]
    return lax.ppermute(value, "mp", pairs)


class Chain:
    def __init__(self, steps, *given):
        next(steps)
        self.steps, self.held, self.done = steps, given, False

    def advance(self):
        if not self.done:
            try:
                self.held = self.steps.send(self.held)
            except StopIteration as stop:
                self.held, self.done = stop.value, True


def fence(chains, *values):
    held, values = lax.optimization_barrier(([c.held for c in chains], values))
    for chain, value in zip(chains, held):
        chain.held = value
    return values


def group_order(groups):
    bits = [1 << b for b in range(groups.bit_length() - 1)]
    orders = []
    for c in range(CORES):
        held = [0]
        for bit in bits if c == 0 else bits[::-1]:
            held = held + [j ^ bit for j in held]
        orders.append(held)
    return orders


def group_pairs(ups, groups, members):
    return [
        (g * members + m, (g ^ ups[m % CORES]) * members + m)
        for g in range(groups)
        for m in range(members)
    ]


def gather_groups(groups, members, held, *plan):
    held += yield
    bits = [1 << b for b in range(groups.bit_length() - 1)]
    steps = list(zip(bits, bits[::-1]))
    for labels in plan:
        first = len(held)
        for label in labels:
            top = label.bit_length() - 1
            pairs = group_pairs(steps[top], groups, members)
            held.append(lax.ppermute(held[label - (1 << top)], ("dp", "mp"), pairs))
        held[first:] = yield held[first:]
    return ()


def exchange_groups(groups, members, mine, theirs):
    blocks = yield
    mine.update(enumerate(blocks, 1))
    bits = [1 << b for b in range(groups.bit_length() - 1)]
    ways = [group_pairs(ups, groups, members) for ups in zip(bits, bits[::-1])]
    left = {at: [w for b, w in zip(bits, ways) if at & b] for at in mine}
    while len(theirs) < len(mine):
        moved = [at for at in mine if left[at]]
        ready = [at for at in mine if not left[at] and at not in theirs]
        came = yield (
            [lax.ppermute(mine[at], ("dp", "mp"), left[at].pop(0)) for at in moved],
            [swap_cores(mine[at], members // CORES) for at in ready],
        )
        mine.update(zip(moved, came[0]))
        theirs.update(zip(ready, came[1]))
    return ()


def on_device(groups, members, tokens, w_gate, w_up, w_down, cotangent):
    group = lax.axis_index("dp")
    place = lax.axis_index("mp") // CORES
    core = lax.rem(lax.axis_index("mp"), CORES)
    where = jnp.stack([place, core, group])
    width = tokens.shape[1] // groups
    phases = groups.bit_length() - 1
    last = groups - 1

    def from_line(value):
        return lax.all_gather(value, "mp", axis=0, tiled=True)

    def over_line(value):
        return lax.psum_scatter(value, "mp", scatter_dimension=0, tiled=True)

    def over_groups(value, held, *plan):
        return Chain(gather_groups(groups, members, held, *plan), value)

    def exchange(blocks, mine, theirs):
        return Chain(exchange_groups(groups, members, mine, theirs), *blocks)

    def columns(gathered, mine, theirs):
        labels = range(1, groups)
        return (gathered, *(mine[at] for at in labels), *(theirs[at] for at in labels))

    upstream = from_line(cotangent)
    (gathered,) = fence([], from_line(tokens))

    blocks = hand_out(where, gathered, groups)
    all_hidden, mine, theirs = [], {}, {}
    across = exchange(blocks, mine, theirs)
    across.advance()
    hidden, swish, slope = fence(
        [across], *forward(after(gathered, blocks), w_gate, w_up)
    )

    hiddens = over_groups(hidden, all_hidden, [1], range(2, last), [last])
    hiddens.advance()
    for _ in range(phases - 1):
        across.advance()
    (partial,) = fence([hiddens, across], project(hidden, w_down))

    hiddens.advance()
    upstream, partial = fence([across], upstream, partial)
    mixed = over_line(partial)

    blocks = hand_out(where, upstream, groups)
    all_dgate, all_dup, mine_up, theirs_up = [], [], {}, {}
    across_up = exchange(blocks, mine_up, theirs_up)
    across_up.advance()
    dgate, dup = backward(after(upstream, blocks), w_down, swish, slope)
    dgate, dup = fence([hiddens, across, across_up], dgate, dup)

    gates = over_groups(dgate, all_dgate, [1], range(2, groups))
    ups = over_groups(dup, all_dup, [1], range(2, groups))
    hiddens.advance()
    gates.advance()
    ups.advance()
    for _ in range(phases - 1):
        across_up.advance()
    (partial,) = fence(
        [gates, ups, hiddens, across, across_up],
        input_sum(dgate, dup, w_gate, w_up),
    )
    input_grad = over_line(partial)

    hiddens.advance()
    gates.advance()
    ups.advance()
    across.advance()
    across_up.advance()
    (mark,) = fence([hiddens, across, across_up], partial)
    across.advance()
    across_up.advance()

    depth = groups * hidden.shape[0]
    shape = (width, hidden.shape[1])
    plans = (columns_plan, pieces_plan)
    grad_down = gradient(
        where,
        plans[::-1],
        after(all_hidden, mark),
        columns(upstream, mine_up, theirs_up),
        depth,
        shape[::-1],
    )
    (grad_down,) = fence([gates], grad_down)
    gates.advance()

    ins = after(columns(gathered, mine, theirs), grad_down)
    grad_gate = gradient(where, plans, ins, all_dgate, depth, shape)
    (grad_gate,) = fence([ups], grad_gate)
    ups.advance()
    grad_up = gradient(where, plans, after(ins, grad_gate), all_dup, depth, shape)
    return mixed, input_grad, grad_gate, grad_up, grad_down


def solution(mesh):
    in_specs = (
        P(("dp", "mp"), None),
        P(None, "mp"),
        P(None, "mp"),
        P("mp", None),
        P(("dp", "mp"), None),
    )
    out_specs = (
        P(("dp", "mp"), None),
        P(("dp", "mp"), None),
        P("dp", "mp"),
        P("dp", "mp"),
        P("mp", "dp"),
    )
    body = functools.partial(on_device, mesh.shape["dp"], mesh.shape["mp"])
    return jax.shard_map(
        body, mesh=mesh, in_specs=in_specs, out_specs=out_specs, check_vma=False
    )
```

```python
import functools

import jax
import jax.numpy as jnp
from jax import lax
from jax.experimental import pallas as pl
from jax.experimental.pallas import tpu as pltpu
from jax.sharding import PartitionSpec as P

CORES = 2
MIB = 1 << 20


def contract_rows(left, right):
    return lax.dot_general(
        left, right, (((0,), (0,)), ((), ())), preferred_element_type=jnp.float32
    )


def contract_cols(left, right):
    return lax.dot_general(
        left, right, (((1,), (1,)), ((), ())), preferred_element_type=jnp.float32
    )


def product(left, right):
    return jnp.dot(left, right, preferred_element_type=jnp.float32)


def after(value, earlier):
    return lax.optimization_barrier((value, earlier))[0]


SMEM = pl.BlockSpec(memory_space=pltpu.SMEM)
ANY = pl.BlockSpec(memory_space=pl.ANY)


def call(body, steps, ins, in_specs, outs, out_specs, scratch=()):
    return pl.pallas_call(
        body,
        grid=(steps,),
        in_specs=in_specs,
        out_specs=out_specs,
        out_shape=outs,
        scratch_shapes=scratch,
        compiler_params=pltpu.CompilerParams(vmem_limit_bytes=56 * MIB),
        cost_estimate=pl.CostEstimate(flops=0, bytes_accessed=0, transcendentals=0),
    )(*ins)


def whole(array):
    return pl.BlockSpec(array.shape, lambda i: (0,) * len(array.shape))


def out_columns(rows, width):
    return jax.ShapeDtypeStruct((rows, width), jnp.bfloat16)


CHUNK = 64
AHEAD = 2
SPLIT = 2


class Stream:
    def __init__(self, weights, axis, block):
        self.axis, self.block, self.count = axis, block, len(weights)
        self.steps = weights[0].shape[axis] // block
        shape = list(weights[0].shape)
        shape[axis] = block
        slots = (self.count, self.steps)
        self.scratch = (
            pltpu.VMEM((*slots, *shape), weights[0].dtype),
            pltpu.SemaphoreType.DMA((*slots, SPLIT)),
        )

    def copies(self, step, refs, held, sems):
        at = step * self.block
        at = pl.ds(at if isinstance(at, int) else pl.multiple_of(at, self.block), self.block)
        rows = held.shape[2] // SPLIT
        for w, ref in enumerate(refs):
            block = ref.at[:, at] if self.axis else ref.at[at]
            for part in range(SPLIT):
                some = pl.ds(part * rows, rows)
                yield pltpu.make_async_copy(
                    block.at[some], held.at[w, step, some], sems.at[w, step, part]
                )

    def begin(self, refs, held, sems, steps):
        for step in steps:
            for copy in self.copies(step, refs, held, sems):
                copy.start()

    def blocks(self, refs, held, sems):
        step = pl.program_id(0)

        @pl.when(step + AHEAD < self.steps)
        def _():
            for copy in self.copies(step + AHEAD, refs, held, sems):
                copy.start()

        for copy in self.copies(step, refs, held, sems):
            copy.wait()
        return [held[w, step] for w in range(self.count)]


class Gathered:
    def __init__(self, rows):
        self.rows = rows
        self.scratch = (
            pltpu.VMEM(rows.shape, rows.dtype),
            pltpu.SemaphoreType.DMA((rows.shape[0] // CHUNK,)),
        )

    def fill(self, ref, x_ref, sems, then):
        copies = []
        for i in range(x_ref.shape[0] // CHUNK):
            at = pl.ds(i * CHUNK, CHUNK)
            copies.append(pltpu.make_async_copy(ref.at[at], x_ref.at[at], sems.at[i]))
        for copy in copies:
            copy.start()
        then()
        for copy in copies:
            copy.wait()


def hand_out_body(orders, where_ref, rows_ref, *refs):
    *outs, sems = refs
    core, group = where_ref[1], where_ref[2]
    copies = []
    for out, j0, j1 in zip(outs, orders[0][1:], orders[1][1:]):
        half, width = out.shape
        at = (group ^ jnp.where(core == 0, j0, j1)) * width
        at = pl.ds(pl.multiple_of(at, width), width)
        rows = pl.ds(pl.multiple_of(core * half, half), half)
        copies.append(
            pltpu.make_async_copy(rows_ref.at[rows, at], out, sems.at[len(copies)])
        )
    for copy in copies:
        copy.start()
    for copy in copies:
        copy.wait()


def hand_out(where, rows, groups):
    block = out_columns(rows.shape[0] // CORES, rows.shape[1] // groups)
    count = groups - 1
    return call(
        functools.partial(hand_out_body, group_order(groups)),
        1,
        (where, rows),
        [SMEM, ANY],
        (block,) * count,
        (whole(block),) * count,
        (pltpu.SemaphoreType.DMA((count,)),),
    )


def forward_body(
    rows, weights, x_in, w_gate_ref, w_up_ref, hidden_ref, swish_ref, slope_ref, *scratch
):
    x_ref, x_sems, held, sems = scratch
    refs = (w_gate_ref, w_up_ref)

    @pl.when(pl.program_id(0) == 0)
    def _():
        weights.begin(refs, held, sems, [0])
        rest = range(1, min(AHEAD, weights.steps))
        rows.fill(x_in, x_ref, x_sems, lambda: weights.begin(refs, held, sems, rest))

    w_gate, w_up = weights.blocks(refs, held, sems)
    gate = product(x_ref[...], w_gate)
    up = product(x_ref[...], w_up)
    sigma = jax.nn.sigmoid(gate)
    swish = gate * sigma
    hidden_ref[...] = (swish * up).astype(hidden_ref.dtype)
    swish_ref[...] = swish
    slope_ref[...] = up * sigma * (1.0 + gate * (1.0 - sigma))


def forward(x, w_gate, w_up):
    rows, panel = x.shape[0], w_gate.shape[1]
    held, weights = Gathered(x), Stream((w_gate, w_up), 1, min(256, panel))
    out = pl.BlockSpec((rows, weights.block), lambda i: (0, i))
    kept = jax.ShapeDtypeStruct((rows, panel), jnp.float32)
    return call(
        functools.partial(forward_body, held, weights),
        weights.steps,
        (x, w_gate, w_up),
        [ANY] * 3,
        (out_columns(rows, panel), kept, kept),
        (out, out, out),
        held.scratch + weights.scratch,
    )


def project_body(weights, hidden_ref, w_ref, out_ref, held, sems):
    steps = range(min(AHEAD, weights.steps))
    pl.when(pl.program_id(0) == 0)(lambda: weights.begin((w_ref,), held, sems, steps))
    (w,) = weights.blocks((w_ref,), held, sems)
    out_ref[...] = product(hidden_ref[...], w).astype(out_ref.dtype)


def project(hidden, w_down):
    rows, depth = hidden.shape[0], w_down.shape[1]
    weights = Stream((w_down,), 1, min(1024, depth))
    return call(
        functools.partial(project_body, weights),
        weights.steps,
        (hidden, w_down),
        [whole(hidden), ANY],
        (jax.ShapeDtypeStruct((rows, depth), jnp.bfloat16),),
        (pl.BlockSpec((rows, weights.block), lambda i: (0, i)),),
        weights.scratch,
    )[0]


def backward_body(
    rows, weights, x_in, w_ref, swish_ref, slope_ref, dgate_ref, dup_ref, *scratch
):
    x_ref, x_sems, held, sems = scratch

    @pl.when(pl.program_id(0) == 0)
    def _():
        weights.begin((w_ref,), held, sems, [0])
        rest = range(1, min(AHEAD, weights.steps))
        rows.fill(
            x_in, x_ref, x_sems, lambda: weights.begin((w_ref,), held, sems, rest)
        )

    (w,) = weights.blocks((w_ref,), held, sems)
    dhidden = contract_cols(x_ref[...], w)
    dgate_ref[...] = (dhidden * slope_ref[...]).astype(dgate_ref.dtype)
    dup_ref[...] = (dhidden * swish_ref[...]).astype(dup_ref.dtype)


def backward(x, w_down, swish, slope):
    rows, panel = x.shape[0], w_down.shape[0]
    held, weights = Gathered(x), Stream((w_down,), 0, min(256, panel))
    part = pl.BlockSpec((rows, weights.block), lambda i: (0, i))
    return call(
        functools.partial(backward_body, held, weights),
        weights.steps,
        (x, w_down, swish, slope),
        [ANY, ANY, part, part],
        (out_columns(rows, panel),) * 2,
        (part, part),
        held.scratch + weights.scratch,
    )


def input_body(weights, dgate_ref, dup_ref, w_gate_ref, w_up_ref, out_ref, held, sems):
    refs = (w_gate_ref, w_up_ref)
    steps = range(min(AHEAD, weights.steps))
    pl.when(pl.program_id(0) == 0)(lambda: weights.begin(refs, held, sems, steps))
    w_gate, w_up = weights.blocks(refs, held, sems)
    total = contract_cols(dgate_ref[...], w_gate) + contract_cols(dup_ref[...], w_up)
    out_ref[...] = total.astype(out_ref.dtype)


def input_sum(dgate, dup, w_gate, w_up):
    rows, depth = dgate.shape[0], w_gate.shape[0]
    weights = Stream((w_gate, w_up), 0, min(1024, depth))
    return call(
        functools.partial(input_body, weights),
        weights.steps,
        (dgate, dup, w_gate, w_up),
        [whole(dgate), whole(dup), ANY, ANY],
        (jax.ShapeDtypeStruct((rows, depth), jnp.bfloat16),),
        (pl.BlockSpec((rows, weights.block), lambda i: (0, i)),),
        weights.scratch,
    )[0]


def gradient_body(plans, counts, where_ref, *refs):
    out_ref, left_ref, right_ref, sems = refs[-4:]

    @pl.when(pl.program_id(0) == 0)
    def _():
        copies, first = [], 0
        for plan, count, held in zip(plans, counts, (left_ref, right_ref)):
            for source, at in plan(where_ref, *refs[first : first + count]):
                rows = source.shape[0]
                target = held.at[pl.ds(pl.multiple_of(at, 16), rows)]
                copies.append(
                    pltpu.make_async_copy(source, target, sems.at[len(copies)])
                )
            first += count
        for copy in copies:
            copy.start()
        for copy in copies:
            copy.wait()

    block = out_ref.shape[0]
    at = pl.ds(pl.multiple_of(pl.program_id(0) * block, block), block)
    total = contract_rows(left_ref[:, at], right_ref[...])
    out_ref[...] = total.astype(out_ref.dtype)


def gradient(where, plans, lefts, rights, depth, shape):
    block = min(256, shape[0])
    counts = (len(lefts), len(rights))
    return call(
        functools.partial(gradient_body, plans, counts),
        shape[0] // block,
        (where, *lefts, *rights),
        [SMEM] + [ANY] * sum(counts),
        (jax.ShapeDtypeStruct(shape, jnp.bfloat16),),
        (pl.BlockSpec((block, shape[1]), lambda i: (i, 0)),),
        (
            pltpu.VMEM((depth, shape[0]), jnp.bfloat16),
            pltpu.VMEM((depth, shape[1]), jnp.bfloat16),
            pltpu.SemaphoreType.DMA((32,)),
        ),
    )[0]


def pieces_plan(where_ref, *pieces):
    copies, at = [], 0
    for piece in pieces:
        copies.append((piece, at))
        at += piece.shape[0]
    return copies


def columns_plan(where_ref, gathered, *blocks):
    core, group, count = where_ref[1], where_ref[2], len(blocks) // 2
    rows, half, width = gathered.shape[0], *blocks[0].shape
    at = pl.ds(pl.multiple_of(group * width, width), width)
    copies = [(gathered.at[:, at], 0)]
    for label in range(1, count + 1):
        mine = blocks[label - 1]
        theirs = blocks[count + reverse(label, count + 1) - 1]
        copies.append((mine, label * rows + core * half))
        copies.append((theirs, label * rows + (1 - core) * half))
    return copies


def reverse(label, count):
    bits = count.bit_length() - 1
    return sum(1 << (bits - 1 - b) for b in range(bits) if label >> b & 1)


def swap_cores(value, chips):
    pairs = [(i, i ^ 1) for i in range(CORES * chips)]
    return lax.ppermute(value, "mp", pairs)


class Chain:
    def __init__(self, steps, *given):
        next(steps)
        self.steps, self.held, self.done = steps, given, False

    def advance(self):
        if not self.done:
            try:
                self.held = self.steps.send(self.held)
            except StopIteration as stop:
                self.held, self.done = stop.value, True


def fence(chains, *values):
    held, values = lax.optimization_barrier(([c.held for c in chains], values))
    for chain, value in zip(chains, held):
        chain.held = value
    return values


def group_order(groups):
    bits = [1 << b for b in range(groups.bit_length() - 1)]
    orders = []
    for c in range(CORES):
        held = [0]
        for bit in bits if c == 0 else bits[::-1]:
            held = held + [j ^ bit for j in held]
        orders.append(held)
    return orders


def group_pairs(ups, groups, members):
    return [
        (g * members + m, (g ^ ups[m % CORES]) * members + m)
        for g in range(groups)
        for m in range(members)
    ]


def gather_groups(groups, members, held, *plan):
    held += yield
    bits = [1 << b for b in range(groups.bit_length() - 1)]
    steps = list(zip(bits, bits[::-1]))
    for labels in plan:
        first = len(held)
        for label in labels:
            top = label.bit_length() - 1
            pairs = group_pairs(steps[top], groups, members)
            held.append(lax.ppermute(held[label - (1 << top)], ("dp", "mp"), pairs))
        held[first:] = yield held[first:]
    return ()


def exchange_groups(groups, members, mine, theirs):
    blocks = yield
    mine.update(enumerate(blocks, 1))
    bits = [1 << b for b in range(groups.bit_length() - 1)]
    ways = [group_pairs(ups, groups, members) for ups in zip(bits, bits[::-1])]
    left = {at: [w for b, w in zip(bits, ways) if at & b] for at in mine}
    while len(theirs) < len(mine):
        moved = [at for at in mine if left[at]]
        ready = [at for at in mine if not left[at] and at not in theirs]
        came = yield (
            [lax.ppermute(mine[at], ("dp", "mp"), left[at].pop(0)) for at in moved],
            [swap_cores(mine[at], members // CORES) for at in ready],
        )
        mine.update(zip(moved, came[0]))
        theirs.update(zip(ready, came[1]))
    return ()


def on_device(groups, members, tokens, w_gate, w_up, w_down, cotangent):
    group = lax.axis_index("dp")
    place = lax.axis_index("mp") // CORES
    core = lax.rem(lax.axis_index("mp"), CORES)
    where = jnp.stack([place, core, group])
    width = tokens.shape[1] // groups
    phases = groups.bit_length() - 1
    last = groups - 1

    def from_line(value):
        return lax.all_gather(value, "mp", axis=0, tiled=True)

    def over_line(value):
        return lax.psum_scatter(value, "mp", scatter_dimension=0, tiled=True)

    def over_groups(value, held, *plan):
        return Chain(gather_groups(groups, members, held, *plan), value)

    def exchange(blocks, mine, theirs):
        return Chain(exchange_groups(groups, members, mine, theirs), *blocks)

    def columns(gathered, mine, theirs):
        labels = range(1, groups)
        return (gathered, *(mine[at] for at in labels), *(theirs[at] for at in labels))

    upstream = from_line(cotangent)
    (gathered,) = fence([], from_line(tokens))

    blocks = hand_out(where, gathered, groups)
    all_hidden, mine, theirs = [], {}, {}
    across = exchange(blocks, mine, theirs)
    across.advance()
    hidden, swish, slope = fence(
        [across], *forward(after(gathered, blocks), w_gate, w_up)
    )

    hiddens = over_groups(hidden, all_hidden, [1], range(2, last), [last])
    hiddens.advance()
    for _ in range(phases - 1):
        across.advance()
    (partial,) = fence([hiddens, across], project(hidden, w_down))

    hiddens.advance()
    upstream, partial = fence([across], upstream, partial)
    mixed = over_line(partial)

    blocks = hand_out(where, upstream, groups)
    all_dgate, all_dup, mine_up, theirs_up = [], [], {}, {}
    across_up = exchange(blocks, mine_up, theirs_up)
    across_up.advance()
    dgate, dup = backward(after(upstream, blocks), w_down, swish, slope)
    dgate, dup = fence([hiddens, across, across_up], dgate, dup)

    gates = over_groups(dgate, all_dgate, [1], range(2, groups))
    ups = over_groups(dup, all_dup, [1], range(2, groups))
    gates.advance()
    ups.advance()
    for _ in range(phases - 1):
        across_up.advance()
    (partial,) = fence(
        [gates, ups, across, across_up],
        input_sum(dgate, dup, w_gate, w_up),
    )
    input_grad = over_line(partial)

    hiddens.advance()
    gates.advance()
    ups.advance()
    across.advance()
    across_up.advance()
    (mark,) = fence([hiddens, across, across_up], partial)
    across.advance()
    across_up.advance()

    depth = groups * hidden.shape[0]
    shape = (width, hidden.shape[1])
    plans = (columns_plan, pieces_plan)
    grad_down = gradient(
        where,
        plans[::-1],
        after(all_hidden, mark),
        columns(upstream, mine_up, theirs_up),
        depth,
        shape[::-1],
    )
    (grad_down,) = fence([gates], grad_down)
    gates.advance()

    ins = after(columns(gathered, mine, theirs), grad_down)
    grad_gate = gradient(where, plans, ins, all_dgate, depth, shape)
    (grad_gate,) = fence([ups], grad_gate)
    ups.advance()
    grad_up = gradient(where, plans, after(ins, grad_gate), all_dup, depth, shape)
    return mixed, input_grad, grad_gate, grad_up, grad_down


def solution(mesh):
    in_specs = (
        P(("dp", "mp"), None),
        P(None, "mp"),
        P(None, "mp"),
        P("mp", None),
        P(("dp", "mp"), None),
    )
    out_specs = (
        P(("dp", "mp"), None),
        P(("dp", "mp"), None),
        P("dp", "mp"),
        P("dp", "mp"),
        P("mp", "dp"),
    )
    body = functools.partial(on_device, mesh.shape["dp"], mesh.shape["mp"])
    return jax.shard_map(
        body, mesh=mesh, in_specs=in_specs, out_specs=out_specs, check_vma=False
    )
```

```python
import functools

import jax
import jax.numpy as jnp
from jax import lax
from jax.experimental import pallas as pl
from jax.experimental.pallas import tpu as pltpu
from jax.sharding import PartitionSpec as P

CORES = 2
MIB = 1 << 20


def contract_rows(left, right):
    return lax.dot_general(
        left, right, (((0,), (0,)), ((), ())), preferred_element_type=jnp.float32
    )


def contract_cols(left, right):
    return lax.dot_general(
        left, right, (((1,), (1,)), ((), ())), preferred_element_type=jnp.float32
    )


def product(left, right):
    return jnp.dot(left, right, preferred_element_type=jnp.float32)


def after(value, earlier):
    return lax.optimization_barrier((value, earlier))[0]


SMEM = pl.BlockSpec(memory_space=pltpu.SMEM)
ANY = pl.BlockSpec(memory_space=pl.ANY)


def call(body, steps, ins, in_specs, outs, out_specs, scratch=()):
    return pl.pallas_call(
        body,
        grid=(steps,),
        in_specs=in_specs,
        out_specs=out_specs,
        out_shape=outs,
        scratch_shapes=scratch,
        compiler_params=pltpu.CompilerParams(vmem_limit_bytes=56 * MIB),
        cost_estimate=pl.CostEstimate(flops=0, bytes_accessed=0, transcendentals=0),
    )(*ins)


def whole(array):
    return pl.BlockSpec(array.shape, lambda i: (0,) * len(array.shape))


def out_columns(rows, width):
    return jax.ShapeDtypeStruct((rows, width), jnp.bfloat16)


CHUNK = 64
AHEAD = 2
SPLIT = 2


class Stream:
    def __init__(self, weights, axis, block):
        self.axis, self.block, self.count = axis, block, len(weights)
        self.steps = weights[0].shape[axis] // block
        shape = list(weights[0].shape)
        shape[axis] = block
        slots = (self.count, self.steps)
        self.scratch = (
            pltpu.VMEM((*slots, *shape), weights[0].dtype),
            pltpu.SemaphoreType.DMA((*slots, SPLIT)),
        )

    def copies(self, step, refs, held, sems):
        at = step * self.block
        at = pl.ds(at if isinstance(at, int) else pl.multiple_of(at, self.block), self.block)
        rows = held.shape[2] // SPLIT
        for w, ref in enumerate(refs):
            block = ref.at[:, at] if self.axis else ref.at[at]
            for part in range(SPLIT):
                some = pl.ds(part * rows, rows)
                yield pltpu.make_async_copy(
                    block.at[some], held.at[w, step, some], sems.at[w, step, part]
                )

    def begin(self, refs, held, sems, steps):
        for step in steps:
            for copy in self.copies(step, refs, held, sems):
                copy.start()

    def blocks(self, refs, held, sems):
        step = pl.program_id(0)

        @pl.when(step + AHEAD < self.steps)
        def _():
            for copy in self.copies(step + AHEAD, refs, held, sems):
                copy.start()

        for copy in self.copies(step, refs, held, sems):
            copy.wait()
        return [held[w, step] for w in range(self.count)]


class Gathered:
    def __init__(self, rows):
        self.rows = rows
        self.scratch = (
            pltpu.VMEM(rows.shape, rows.dtype),
            pltpu.SemaphoreType.DMA((rows.shape[0] // CHUNK,)),
        )

    def fill(self, ref, x_ref, sems, then):
        copies = []
        for i in range(x_ref.shape[0] // CHUNK):
            at = pl.ds(i * CHUNK, CHUNK)
            copies.append(pltpu.make_async_copy(ref.at[at], x_ref.at[at], sems.at[i]))
        for copy in copies:
            copy.start()
        then()
        for copy in copies:
            copy.wait()


def hand_out_body(orders, where_ref, rows_ref, *refs):
    *outs, sems = refs
    core, group = where_ref[1], where_ref[2]
    copies = []
    for out, j0, j1 in zip(outs, orders[0][1:], orders[1][1:]):
        half, width = out.shape
        at = (group ^ jnp.where(core == 0, j0, j1)) * width
        at = pl.ds(pl.multiple_of(at, width), width)
        rows = pl.ds(pl.multiple_of(core * half, half), half)
        copies.append(
            pltpu.make_async_copy(rows_ref.at[rows, at], out, sems.at[len(copies)])
        )
    for copy in copies:
        copy.start()
    for copy in copies:
        copy.wait()


def hand_out(where, rows, groups):
    block = out_columns(rows.shape[0] // CORES, rows.shape[1] // groups)
    count = groups - 1
    return call(
        functools.partial(hand_out_body, group_order(groups)),
        1,
        (where, rows),
        [SMEM, ANY],
        (block,) * count,
        (whole(block),) * count,
        (pltpu.SemaphoreType.DMA((count,)),),
    )


def forward_body(
    rows, weights, x_in, w_gate_ref, w_up_ref, hidden_ref, swish_ref, slope_ref, *scratch
):
    x_ref, x_sems, held, sems = scratch
    refs = (w_gate_ref, w_up_ref)

    @pl.when(pl.program_id(0) == 0)
    def _():
        weights.begin(refs, held, sems, [0])
        rest = range(1, min(AHEAD, weights.steps))
        rows.fill(x_in, x_ref, x_sems, lambda: weights.begin(refs, held, sems, rest))

    w_gate, w_up = weights.blocks(refs, held, sems)
    gate = product(x_ref[...], w_gate)
    up = product(x_ref[...], w_up)
    sigma = jax.nn.sigmoid(gate)
    swish = gate * sigma
    hidden_ref[...] = (swish * up).astype(hidden_ref.dtype)
    swish_ref[...] = swish
    slope_ref[...] = up * sigma * (1.0 + gate * (1.0 - sigma))


def forward(x, w_gate, w_up):
    rows, panel = x.shape[0], w_gate.shape[1]
    held, weights = Gathered(x), Stream((w_gate, w_up), 1, min(256, panel))
    out = pl.BlockSpec((rows, weights.block), lambda i: (0, i))
    kept = jax.ShapeDtypeStruct((rows, panel), jnp.float32)
    return call(
        functools.partial(forward_body, held, weights),
        weights.steps,
        (x, w_gate, w_up),
        [ANY] * 3,
        (out_columns(rows, panel), kept, kept),
        (out, out, out),
        held.scratch + weights.scratch,
    )


def project_body(weights, hidden_ref, w_ref, out_ref, held, sems):
    steps = range(min(AHEAD, weights.steps))
    pl.when(pl.program_id(0) == 0)(lambda: weights.begin((w_ref,), held, sems, steps))
    (w,) = weights.blocks((w_ref,), held, sems)
    out_ref[...] = product(hidden_ref[...], w).astype(out_ref.dtype)


def project(hidden, w_down):
    rows, depth = hidden.shape[0], w_down.shape[1]
    weights = Stream((w_down,), 1, min(1024, depth))
    return call(
        functools.partial(project_body, weights),
        weights.steps,
        (hidden, w_down),
        [whole(hidden), ANY],
        (jax.ShapeDtypeStruct((rows, depth), jnp.bfloat16),),
        (pl.BlockSpec((rows, weights.block), lambda i: (0, i)),),
        weights.scratch,
    )[0]


def backward_body(
    rows, weights, x_in, w_ref, swish_ref, slope_ref, dgate_ref, dup_ref, *scratch
):
    x_ref, x_sems, held, sems = scratch

    @pl.when(pl.program_id(0) == 0)
    def _():
        weights.begin((w_ref,), held, sems, [0])
        rest = range(1, min(AHEAD, weights.steps))
        rows.fill(
            x_in, x_ref, x_sems, lambda: weights.begin((w_ref,), held, sems, rest)
        )

    (w,) = weights.blocks((w_ref,), held, sems)
    dhidden = contract_cols(x_ref[...], w)
    dgate_ref[...] = (dhidden * slope_ref[...]).astype(dgate_ref.dtype)
    dup_ref[...] = (dhidden * swish_ref[...]).astype(dup_ref.dtype)


def backward(x, w_down, swish, slope):
    rows, panel = x.shape[0], w_down.shape[0]
    held, weights = Gathered(x), Stream((w_down,), 0, min(256, panel))
    part = pl.BlockSpec((rows, weights.block), lambda i: (0, i))
    return call(
        functools.partial(backward_body, held, weights),
        weights.steps,
        (x, w_down, swish, slope),
        [ANY, ANY, part, part],
        (out_columns(rows, panel),) * 2,
        (part, part),
        held.scratch + weights.scratch,
    )


def input_body(weights, dgate_ref, dup_ref, w_gate_ref, w_up_ref, out_ref, held, sems):
    refs = (w_gate_ref, w_up_ref)
    steps = range(min(AHEAD, weights.steps))
    pl.when(pl.program_id(0) == 0)(lambda: weights.begin(refs, held, sems, steps))
    w_gate, w_up = weights.blocks(refs, held, sems)
    total = contract_cols(dgate_ref[...], w_gate) + contract_cols(dup_ref[...], w_up)
    out_ref[...] = total.astype(out_ref.dtype)


def input_sum(dgate, dup, w_gate, w_up):
    rows, depth = dgate.shape[0], w_gate.shape[0]
    weights = Stream((w_gate, w_up), 0, min(1024, depth))
    return call(
        functools.partial(input_body, weights),
        weights.steps,
        (dgate, dup, w_gate, w_up),
        [whole(dgate), whole(dup), ANY, ANY],
        (jax.ShapeDtypeStruct((rows, depth), jnp.bfloat16),),
        (pl.BlockSpec((rows, weights.block), lambda i: (0, i)),),
        weights.scratch,
    )[0]


def gradient_body(plans, counts, where_ref, *refs):
    out_ref, left_ref, right_ref, sems = refs[-4:]

    @pl.when(pl.program_id(0) == 0)
    def _():
        copies, first = [], 0
        for plan, count, held in zip(plans, counts, (left_ref, right_ref)):
            for source, at in plan(where_ref, *refs[first : first + count]):
                rows = source.shape[0]
                target = held.at[pl.ds(pl.multiple_of(at, 16), rows)]
                copies.append(
                    pltpu.make_async_copy(source, target, sems.at[len(copies)])
                )
            first += count
        for copy in copies:
            copy.start()
        for copy in copies:
            copy.wait()

    block = out_ref.shape[0]
    at = pl.ds(pl.multiple_of(pl.program_id(0) * block, block), block)
    total = contract_rows(left_ref[:, at], right_ref[...])
    out_ref[...] = total.astype(out_ref.dtype)


def gradient(where, plans, lefts, rights, depth, shape):
    block = min(256, shape[0])
    counts = (len(lefts), len(rights))
    return call(
        functools.partial(gradient_body, plans, counts),
        shape[0] // block,
        (where, *lefts, *rights),
        [SMEM] + [ANY] * sum(counts),
        (jax.ShapeDtypeStruct(shape, jnp.bfloat16),),
        (pl.BlockSpec((block, shape[1]), lambda i: (i, 0)),),
        (
            pltpu.VMEM((depth, shape[0]), jnp.bfloat16),
            pltpu.VMEM((depth, shape[1]), jnp.bfloat16),
            pltpu.SemaphoreType.DMA((32,)),
        ),
    )[0]


def pieces_plan(where_ref, *pieces):
    copies, at = [], 0
    for piece in pieces:
        copies.append((piece, at))
        at += piece.shape[0]
    return copies


def columns_plan(where_ref, gathered, *blocks):
    core, group, count = where_ref[1], where_ref[2], len(blocks) // 2
    rows, half, width = gathered.shape[0], *blocks[0].shape
    at = pl.ds(pl.multiple_of(group * width, width), width)
    copies = [(gathered.at[:, at], 0)]
    for label in range(1, count + 1):
        mine = blocks[label - 1]
        theirs = blocks[count + reverse(label, count + 1) - 1]
        copies.append((mine, label * rows + core * half))
        copies.append((theirs, label * rows + (1 - core) * half))
    return copies


def reverse(label, count):
    bits = count.bit_length() - 1
    return sum(1 << (bits - 1 - b) for b in range(bits) if label >> b & 1)


def swap_cores(value, chips):
    pairs = [(i, i ^ 1) for i in range(CORES * chips)]
    return lax.ppermute(value, "mp", pairs)


class Chain:
    def __init__(self, steps, *given):
        next(steps)
        self.steps, self.held, self.done = steps, given, False

    def advance(self):
        if not self.done:
            try:
                self.held = self.steps.send(self.held)
            except StopIteration as stop:
                self.held, self.done = stop.value, True


def fence(chains, *values):
    held, values = lax.optimization_barrier(([c.held for c in chains], values))
    for chain, value in zip(chains, held):
        chain.held = value
    return values


def group_order(groups):
    bits = [1 << b for b in range(groups.bit_length() - 1)]
    orders = []
    for c in range(CORES):
        held = [0]
        for bit in bits if c == 0 else bits[::-1]:
            held = held + [j ^ bit for j in held]
        orders.append(held)
    return orders


def group_pairs(ups, groups, members):
    return [
        (g * members + m, (g ^ ups[m % CORES]) * members + m)
        for g in range(groups)
        for m in range(members)
    ]


def gather_groups(groups, members, held, *plan):
    held += yield
    bits = [1 << b for b in range(groups.bit_length() - 1)]
    steps = list(zip(bits, bits[::-1]))
    for labels in plan:
        first = len(held)
        for label in labels:
            top = label.bit_length() - 1
            pairs = group_pairs(steps[top], groups, members)
            held.append(lax.ppermute(held[label - (1 << top)], ("dp", "mp"), pairs))
        held[first:] = yield held[first:]
    return ()


def exchange_groups(groups, members, mine, theirs):
    blocks = yield
    mine.update(enumerate(blocks, 1))
    bits = [1 << b for b in range(groups.bit_length() - 1)]
    ways = [group_pairs(ups, groups, members) for ups in zip(bits, bits[::-1])]
    left = {at: [w for b, w in zip(bits, ways) if at & b] for at in mine}
    while len(theirs) < len(mine):
        moved = [at for at in mine if left[at]]
        ready = [at for at in mine if not left[at] and at not in theirs]
        came = yield (
            [lax.ppermute(mine[at], ("dp", "mp"), left[at].pop(0)) for at in moved],
            [swap_cores(mine[at], members // CORES) for at in ready],
        )
        mine.update(zip(moved, came[0]))
        theirs.update(zip(ready, came[1]))
    return ()


def on_device(groups, members, tokens, w_gate, w_up, w_down, cotangent):
    group = lax.axis_index("dp")
    place = lax.axis_index("mp") // CORES
    core = lax.rem(lax.axis_index("mp"), CORES)
    where = jnp.stack([place, core, group])
    width = tokens.shape[1] // groups
    phases = groups.bit_length() - 1
    last = groups - 1

    def from_line(value):
        return lax.all_gather(value, "mp", axis=0, tiled=True)

    def over_line(value):
        return lax.psum_scatter(value, "mp", scatter_dimension=0, tiled=True)

    def over_groups(value, held, *plan):
        return Chain(gather_groups(groups, members, held, *plan), value)

    def exchange(blocks, mine, theirs):
        return Chain(exchange_groups(groups, members, mine, theirs), *blocks)

    def columns(gathered, mine, theirs):
        labels = range(1, groups)
        return (gathered, *(mine[at] for at in labels), *(theirs[at] for at in labels))

    upstream = from_line(cotangent)
    (gathered,) = fence([], from_line(tokens))

    blocks = hand_out(where, gathered, groups)
    all_hidden, mine, theirs = [], {}, {}
    across = exchange(blocks, mine, theirs)
    across.advance()
    hidden, swish, slope = fence(
        [across], *forward(after(gathered, blocks), w_gate, w_up)
    )

    hiddens = over_groups(hidden, all_hidden, range(1, last), [last])
    hiddens.advance()
    for _ in range(phases - 1):
        across.advance()
    (partial,) = fence([hiddens, across], project(hidden, w_down))

    upstream, partial = fence([across], upstream, partial)
    mixed = over_line(partial)

    blocks = hand_out(where, upstream, groups)
    all_dgate, all_dup, mine_up, theirs_up = [], [], {}, {}
    across_up = exchange(blocks, mine_up, theirs_up)
    across_up.advance()
    dgate, dup = backward(after(upstream, blocks), w_down, swish, slope)
    dgate, dup = fence([hiddens, across, across_up], dgate, dup)

    gates = over_groups(dgate, all_dgate, [1], range(2, groups))
    ups = over_groups(dup, all_dup, [1], range(2, groups))
    hiddens.advance()
    gates.advance()
    for _ in range(phases - 1):
        across_up.advance()
    (partial,) = fence(
        [gates, hiddens, across, across_up], input_sum(dgate, dup, w_gate, w_up)
    )
    input_grad = over_line(partial)

    hiddens.advance()
    gates.advance()
    ups.advance()
    across.advance()
    across_up.advance()
    (mark,) = fence([hiddens, across, across_up], partial)
    across.advance()
    across_up.advance()

    depth = groups * hidden.shape[0]
    shape = (width, hidden.shape[1])
    plans = (columns_plan, pieces_plan)
    grad_down = gradient(
        where,
        plans[::-1],
        after(all_hidden, mark),
        columns(upstream, mine_up, theirs_up),
        depth,
        shape[::-1],
    )
    (grad_down,) = fence([gates, ups], grad_down)
    gates.advance()

    ups.advance()
    ins = after(columns(gathered, mine, theirs), grad_down)
    grad_gate = gradient(where, plans, ins, all_dgate, depth, shape)
    (grad_gate,) = fence([ups], grad_gate)
    ups.advance()
    grad_up = gradient(where, plans, after(ins, grad_gate), all_dup, depth, shape)
    return mixed, input_grad, grad_gate, grad_up, grad_down


def solution(mesh):
    in_specs = (
        P(("dp", "mp"), None),
        P(None, "mp"),
        P(None, "mp"),
        P("mp", None),
        P(("dp", "mp"), None),
    )
    out_specs = (
        P(("dp", "mp"), None),
        P(("dp", "mp"), None),
        P("dp", "mp"),
        P("dp", "mp"),
        P("mp", "dp"),
    )
    body = functools.partial(on_device, mesh.shape["dp"], mesh.shape["mp"])
    return jax.shard_map(
        body, mesh=mesh, in_specs=in_specs, out_specs=out_specs, check_vma=False
    )
```

```python
import functools

import jax
import jax.numpy as jnp
from jax import lax
from jax.experimental import pallas as pl
from jax.experimental.pallas import tpu as pltpu
from jax.sharding import PartitionSpec as P

CORES = 2
MIB = 1 << 20


def contract_rows(left, right):
    return lax.dot_general(
        left, right, (((0,), (0,)), ((), ())), preferred_element_type=jnp.float32
    )


def contract_cols(left, right):
    return lax.dot_general(
        left, right, (((1,), (1,)), ((), ())), preferred_element_type=jnp.float32
    )


def product(left, right):
    return jnp.dot(left, right, preferred_element_type=jnp.float32)


def after(value, earlier):
    return lax.optimization_barrier((value, earlier))[0]


SMEM = pl.BlockSpec(memory_space=pltpu.SMEM)
ANY = pl.BlockSpec(memory_space=pl.ANY)


def call(body, steps, ins, in_specs, outs, out_specs, scratch=()):
    return pl.pallas_call(
        body,
        grid=(steps,),
        in_specs=in_specs,
        out_specs=out_specs,
        out_shape=outs,
        scratch_shapes=scratch,
        compiler_params=pltpu.CompilerParams(vmem_limit_bytes=56 * MIB),
        cost_estimate=pl.CostEstimate(flops=0, bytes_accessed=0, transcendentals=0),
    )(*ins)


def whole(array):
    return pl.BlockSpec(array.shape, lambda i: (0,) * len(array.shape))


def out_columns(rows, width):
    return jax.ShapeDtypeStruct((rows, width), jnp.bfloat16)


CHUNK = 64
AHEAD = 2
SPLIT = 2


class Stream:
    def __init__(self, weights, axis, block):
        self.axis, self.block, self.count = axis, block, len(weights)
        self.steps = weights[0].shape[axis] // block
        shape = list(weights[0].shape)
        shape[axis] = block
        slots = (self.count, self.steps)
        self.scratch = (
            pltpu.VMEM((*slots, *shape), weights[0].dtype),
            pltpu.SemaphoreType.DMA((*slots, SPLIT)),
        )

    def copies(self, step, refs, held, sems):
        at = step * self.block
        at = pl.ds(at if isinstance(at, int) else pl.multiple_of(at, self.block), self.block)
        rows = held.shape[2] // SPLIT
        for w, ref in enumerate(refs):
            block = ref.at[:, at] if self.axis else ref.at[at]
            for part in range(SPLIT):
                some = pl.ds(part * rows, rows)
                yield pltpu.make_async_copy(
                    block.at[some], held.at[w, step, some], sems.at[w, step, part]
                )

    def begin(self, refs, held, sems, steps):
        for step in steps:
            for copy in self.copies(step, refs, held, sems):
                copy.start()

    def blocks(self, refs, held, sems):
        step = pl.program_id(0)

        @pl.when(step + AHEAD < self.steps)
        def _():
            for copy in self.copies(step + AHEAD, refs, held, sems):
                copy.start()

        for copy in self.copies(step, refs, held, sems):
            copy.wait()
        return [held[w, step] for w in range(self.count)]


class Gathered:
    def __init__(self, rows):
        self.rows = rows
        self.scratch = (
            pltpu.VMEM(rows.shape, rows.dtype),
            pltpu.SemaphoreType.DMA((rows.shape[0] // CHUNK,)),
        )

    def fill(self, ref, x_ref, sems, then):
        copies = []
        for i in range(x_ref.shape[0] // CHUNK):
            at = pl.ds(i * CHUNK, CHUNK)
            copies.append(pltpu.make_async_copy(ref.at[at], x_ref.at[at], sems.at[i]))
        for copy in copies:
            copy.start()
        then()
        for copy in copies:
            copy.wait()


def hand_out_body(orders, where_ref, rows_ref, *refs):
    *outs, sems = refs
    core, group = where_ref[1], where_ref[2]
    copies = []
    for out, j0, j1 in zip(outs, orders[0][1:], orders[1][1:]):
        half, width = out.shape
        at = (group ^ jnp.where(core == 0, j0, j1)) * width
        at = pl.ds(pl.multiple_of(at, width), width)
        rows = pl.ds(pl.multiple_of(core * half, half), half)
        copies.append(
            pltpu.make_async_copy(rows_ref.at[rows, at], out, sems.at[len(copies)])
        )
    for copy in copies:
        copy.start()
    for copy in copies:
        copy.wait()


def hand_out(where, rows, groups):
    block = out_columns(rows.shape[0] // CORES, rows.shape[1] // groups)
    count = groups - 1
    return call(
        functools.partial(hand_out_body, group_order(groups)),
        1,
        (where, rows),
        [SMEM, ANY],
        (block,) * count,
        (whole(block),) * count,
        (pltpu.SemaphoreType.DMA((count,)),),
    )


def forward_body(
    rows, weights, x_in, w_gate_ref, w_up_ref, hidden_ref, swish_ref, slope_ref, *scratch
):
    x_ref, x_sems, held, sems = scratch
    refs = (w_gate_ref, w_up_ref)

    @pl.when(pl.program_id(0) == 0)
    def _():
        weights.begin(refs, held, sems, [0])
        rest = range(1, min(AHEAD, weights.steps))
        rows.fill(x_in, x_ref, x_sems, lambda: weights.begin(refs, held, sems, rest))

    w_gate, w_up = weights.blocks(refs, held, sems)
    gate = product(x_ref[...], w_gate)
    up = product(x_ref[...], w_up)
    sigma = jax.nn.sigmoid(gate)
    swish = gate * sigma
    hidden_ref[...] = (swish * up).astype(hidden_ref.dtype)
    swish_ref[...] = swish
    slope_ref[...] = up * sigma * (1.0 + gate * (1.0 - sigma))


def forward(x, w_gate, w_up):
    rows, panel = x.shape[0], w_gate.shape[1]
    held, weights = Gathered(x), Stream((w_gate, w_up), 1, min(256, panel))
    out = pl.BlockSpec((rows, weights.block), lambda i: (0, i))
    kept = jax.ShapeDtypeStruct((rows, panel), jnp.float32)
    return call(
        functools.partial(forward_body, held, weights),
        weights.steps,
        (x, w_gate, w_up),
        [ANY] * 3,
        (out_columns(rows, panel), kept, kept),
        (out, out, out),
        held.scratch + weights.scratch,
    )


def project_body(weights, hidden_ref, w_ref, out_ref, held, sems):
    steps = range(min(AHEAD, weights.steps))
    pl.when(pl.program_id(0) == 0)(lambda: weights.begin((w_ref,), held, sems, steps))
    (w,) = weights.blocks((w_ref,), held, sems)
    out_ref[...] = product(hidden_ref[...], w).astype(out_ref.dtype)


def project(hidden, w_down):
    rows, depth = hidden.shape[0], w_down.shape[1]
    weights = Stream((w_down,), 1, min(1024, depth))
    return call(
        functools.partial(project_body, weights),
        weights.steps,
        (hidden, w_down),
        [whole(hidden), ANY],
        (jax.ShapeDtypeStruct((rows, depth), jnp.bfloat16),),
        (pl.BlockSpec((rows, weights.block), lambda i: (0, i)),),
        weights.scratch,
    )[0]


def backward_body(
    rows, weights, x_in, w_ref, swish_ref, slope_ref, dgate_ref, dup_ref, *scratch
):
    x_ref, x_sems, held, sems = scratch

    @pl.when(pl.program_id(0) == 0)
    def _():
        weights.begin((w_ref,), held, sems, [0])
        rest = range(1, min(AHEAD, weights.steps))
        rows.fill(
            x_in, x_ref, x_sems, lambda: weights.begin((w_ref,), held, sems, rest)
        )

    (w,) = weights.blocks((w_ref,), held, sems)
    dhidden = contract_cols(x_ref[...], w)
    dgate_ref[...] = (dhidden * slope_ref[...]).astype(dgate_ref.dtype)
    dup_ref[...] = (dhidden * swish_ref[...]).astype(dup_ref.dtype)


def backward(x, w_down, swish, slope):
    rows, panel = x.shape[0], w_down.shape[0]
    held, weights = Gathered(x), Stream((w_down,), 0, min(256, panel))
    part = pl.BlockSpec((rows, weights.block), lambda i: (0, i))
    return call(
        functools.partial(backward_body, held, weights),
        weights.steps,
        (x, w_down, swish, slope),
        [ANY, ANY, part, part],
        (out_columns(rows, panel),) * 2,
        (part, part),
        held.scratch + weights.scratch,
    )


def input_body(weights, dgate_ref, dup_ref, w_gate_ref, w_up_ref, out_ref, held, sems):
    refs = (w_gate_ref, w_up_ref)
    steps = range(min(AHEAD, weights.steps))
    pl.when(pl.program_id(0) == 0)(lambda: weights.begin(refs, held, sems, steps))
    w_gate, w_up = weights.blocks(refs, held, sems)
    total = contract_cols(dgate_ref[...], w_gate) + contract_cols(dup_ref[...], w_up)
    out_ref[...] = total.astype(out_ref.dtype)


def input_sum(dgate, dup, w_gate, w_up):
    rows, depth = dgate.shape[0], w_gate.shape[0]
    weights = Stream((w_gate, w_up), 0, min(1024, depth))
    return call(
        functools.partial(input_body, weights),
        weights.steps,
        (dgate, dup, w_gate, w_up),
        [whole(dgate), whole(dup), ANY, ANY],
        (jax.ShapeDtypeStruct((rows, depth), jnp.bfloat16),),
        (pl.BlockSpec((rows, weights.block), lambda i: (0, i)),),
        weights.scratch,
    )[0]


def gradient_body(plans, counts, where_ref, *refs):
    out_ref, left_ref, right_ref, sems = refs[-4:]

    @pl.when(pl.program_id(0) == 0)
    def _():
        copies, first = [], 0
        for plan, count, held in zip(plans, counts, (left_ref, right_ref)):
            for source, at in plan(where_ref, *refs[first : first + count]):
                rows = source.shape[0]
                target = held.at[pl.ds(pl.multiple_of(at, 16), rows)]
                copies.append(
                    pltpu.make_async_copy(source, target, sems.at[len(copies)])
                )
            first += count
        for copy in copies:
            copy.start()
        for copy in copies:
            copy.wait()

    block = out_ref.shape[0]
    at = pl.ds(pl.multiple_of(pl.program_id(0) * block, block), block)
    total = contract_rows(left_ref[:, at], right_ref[...])
    out_ref[...] = total.astype(out_ref.dtype)


def gradient(where, plans, lefts, rights, depth, shape):
    block = min(256, shape[0])
    counts = (len(lefts), len(rights))
    return call(
        functools.partial(gradient_body, plans, counts),
        shape[0] // block,
        (where, *lefts, *rights),
        [SMEM] + [ANY] * sum(counts),
        (jax.ShapeDtypeStruct(shape, jnp.bfloat16),),
        (pl.BlockSpec((block, shape[1]), lambda i: (i, 0)),),
        (
            pltpu.VMEM((depth, shape[0]), jnp.bfloat16),
            pltpu.VMEM((depth, shape[1]), jnp.bfloat16),
            pltpu.SemaphoreType.DMA((32,)),
        ),
    )[0]


def pieces_plan(where_ref, *pieces):
    copies, at = [], 0
    for piece in pieces:
        copies.append((piece, at))
        at += piece.shape[0]
    return copies


def columns_plan(where_ref, gathered, *blocks):
    core, group, count = where_ref[1], where_ref[2], len(blocks) // 2
    rows, half, width = gathered.shape[0], *blocks[0].shape
    at = pl.ds(pl.multiple_of(group * width, width), width)
    copies = [(gathered.at[:, at], 0)]
    for label in range(1, count + 1):
        mine = blocks[label - 1]
        theirs = blocks[count + reverse(label, count + 1) - 1]
        copies.append((mine, label * rows + core * half))
        copies.append((theirs, label * rows + (1 - core) * half))
    return copies


def reverse(label, count):
    bits = count.bit_length() - 1
    return sum(1 << (bits - 1 - b) for b in range(bits) if label >> b & 1)


def swap_cores(value, chips):
    pairs = [(i, i ^ 1) for i in range(CORES * chips)]
    return lax.ppermute(value, "mp", pairs)


class Chain:
    def __init__(self, steps, *given):
        next(steps)
        self.steps, self.held, self.done = steps, given, False

    def advance(self):
        if not self.done:
            try:
                self.held = self.steps.send(self.held)
            except StopIteration as stop:
                self.held, self.done = stop.value, True


def fence(chains, *values):
    held, values = lax.optimization_barrier(([c.held for c in chains], values))
    for chain, value in zip(chains, held):
        chain.held = value
    return values


def group_order(groups):
    bits = [1 << b for b in range(groups.bit_length() - 1)]
    orders = []
    for c in range(CORES):
        held = [0]
        for bit in bits if c == 0 else bits[::-1]:
            held = held + [j ^ bit for j in held]
        orders.append(held)
    return orders


def group_pairs(ups, groups, members):
    return [
        (g * members + m, (g ^ ups[m % CORES]) * members + m)
        for g in range(groups)
        for m in range(members)
    ]


def gather_groups(groups, members, held, *plan):
    held += yield
    bits = [1 << b for b in range(groups.bit_length() - 1)]
    steps = list(zip(bits, bits[::-1]))
    for labels in plan:
        first = len(held)
        for label in labels:
            top = label.bit_length() - 1
            pairs = group_pairs(steps[top], groups, members)
            held.append(lax.ppermute(held[label - (1 << top)], ("dp", "mp"), pairs))
        held[first:] = yield held[first:]
    return ()


def exchange_groups(groups, members, mine, theirs):
    blocks = yield
    mine.update(enumerate(blocks, 1))
    bits = [1 << b for b in range(groups.bit_length() - 1)]
    ways = [group_pairs(ups, groups, members) for ups in zip(bits, bits[::-1])]
    left = {at: [w for b, w in zip(bits, ways) if at & b] for at in mine}
    while len(theirs) < len(mine):
        moved = [at for at in mine if left[at]]
        ready = [at for at in mine if not left[at] and at not in theirs]
        came = yield (
            [lax.ppermute(mine[at], ("dp", "mp"), left[at].pop(0)) for at in moved],
            [swap_cores(mine[at], members // CORES) for at in ready],
        )
        mine.update(zip(moved, came[0]))
        theirs.update(zip(ready, came[1]))
    return ()


def on_device(groups, members, tokens, w_gate, w_up, w_down, cotangent):
    group = lax.axis_index("dp")
    place = lax.axis_index("mp") // CORES
    core = lax.rem(lax.axis_index("mp"), CORES)
    where = jnp.stack([place, core, group])
    width = tokens.shape[1] // groups
    phases = groups.bit_length() - 1
    last = groups - 1

    def from_line(value):
        return lax.all_gather(value, "mp", axis=0, tiled=True)

    def over_line(value):
        return lax.psum_scatter(value, "mp", scatter_dimension=0, tiled=True)

    def over_groups(value, held, *plan):
        return Chain(gather_groups(groups, members, held, *plan), value)

    def exchange(blocks, mine, theirs):
        return Chain(exchange_groups(groups, members, mine, theirs), *blocks)

    def columns(gathered, mine, theirs):
        labels = range(1, groups)
        return (gathered, *(mine[at] for at in labels), *(theirs[at] for at in labels))

    upstream = from_line(cotangent)
    (gathered,) = fence([], from_line(tokens))

    blocks = hand_out(where, gathered, groups)
    all_hidden, mine, theirs = [], {}, {}
    across = exchange(blocks, mine, theirs)
    across.advance()
    hidden, swish, slope = fence(
        [across], *forward(after(gathered, blocks), w_gate, w_up)
    )

    hiddens = over_groups(hidden, all_hidden, range(1, last), [last])
    hiddens.advance()
    for _ in range(phases - 1):
        across.advance()
    (partial,) = fence([hiddens, across], project(hidden, w_down))

    upstream, partial = fence([across], upstream, partial)
    mixed = over_line(partial)

    blocks = hand_out(where, upstream, groups)
    all_dgate, all_dup, mine_up, theirs_up = [], [], {}, {}
    across_up = exchange(blocks, mine_up, theirs_up)
    across_up.advance()
    hiddens.advance()
    dgate, dup = backward(after(upstream, blocks), w_down, swish, slope)
    dgate, dup = fence([hiddens, across, across_up], dgate, dup)
    hiddens.advance()

    gates = over_groups(dgate, all_dgate, [1], range(2, groups))
    ups = over_groups(dup, all_dup, [1], range(2, groups))
    gates.advance()
    ups.advance()
    for _ in range(phases - 1):
        across_up.advance()
    (partial,) = fence(
        [gates, ups, across, across_up],
        input_sum(dgate, dup, w_gate, w_up),
    )
    input_grad = over_line(partial)

    gates.advance()
    ups.advance()
    across.advance()
    across_up.advance()
    (mark,) = fence([across, across_up], partial)
    across.advance()
    across_up.advance()

    depth = groups * hidden.shape[0]
    shape = (width, hidden.shape[1])
    plans = (columns_plan, pieces_plan)
    grad_down = gradient(
        where,
        plans[::-1],
        after(all_hidden, mark),
        columns(upstream, mine_up, theirs_up),
        depth,
        shape[::-1],
    )
    (grad_down,) = fence([gates], grad_down)
    gates.advance()

    ins = after(columns(gathered, mine, theirs), grad_down)
    grad_gate = gradient(where, plans, ins, all_dgate, depth, shape)
    (grad_gate,) = fence([ups], grad_gate)
    ups.advance()
    grad_up = gradient(where, plans, after(ins, grad_gate), all_dup, depth, shape)
    return mixed, input_grad, grad_gate, grad_up, grad_down


def solution(mesh):
    in_specs = (
        P(("dp", "mp"), None),
        P(None, "mp"),
        P(None, "mp"),
        P("mp", None),
        P(("dp", "mp"), None),
    )
    out_specs = (
        P(("dp", "mp"), None),
        P(("dp", "mp"), None),
        P("dp", "mp"),
        P("dp", "mp"),
        P("mp", "dp"),
    )
    body = functools.partial(on_device, mesh.shape["dp"], mesh.shape["mp"])
    return jax.shard_map(
        body, mesh=mesh, in_specs=in_specs, out_specs=out_specs, check_vma=False
    )
```
